1024 devices in a mesh: prow: 16 (over x, z_hi, core), pcol: 64 (over z_lo, y).
Axes of the slice: x: 4, y: 4, z: 32 (z_hi: 2, z_lo: 16; z = z_hi * 16 + z_lo), core: 2. Of those that a mesh axis runs over, the one named last changes fastest.
Arguments:
- left_blocks: bfloat16 [38912, 128, 128], P(('prow', 'pcol')), may hold values from -6 to 6
- left_mask: int32 [38912], P(('prow', 'pcol')), may hold values from 0 to 1, as said below
- right_blocks: bfloat16 [24576, 128, 128], P(('prow', 'pcol')), may hold values from -0.125 to 0.125
- pair_lists: int32 [1024, 4, 3, 12], P(('prow', 'pcol')), may hold values from 0 to 37, as said below
- pair_counts: int32 [1024, 4], P(('prow', 'pcol')), may hold values from 0 to 12, as said below
Outputs:
- product: bfloat16 [4096, 8192], P('prow', 'pcol')
The draws below stay inside these ranges and needn't reach their ends.
Inputs may be any that keep to these rules, and one draw needn't show every extreme that they name: `left_mask`: each process's 38 entries hold between 9 and 19 ones; some process holds exactly 19. `pair_lists`: each slot of a right sub-panel stores one block (k, j) of the right matrix, k < 19 a contraction block of the panel and j < 1 a block column, distinct within the sub-panel (the keys are not given). For process (r, c) and step u with s = u - 2, the live pairs are exactly all pairs of an occupied left block i * 19 + k of the panel of process (r, (c + s) mod 64) with the slot of the step's sub-panel that stores (k, j), each listed once with entry 2 = i + j. Every entry 0, live or not, names an occupied left block of that panel; entry 1 is below 6; entry 2 is below 2. `pair_counts`: some process has 12 live pairs in every step.
All inputs are finite; a program needn't handle non-finite values.
Results may differ from the reference program's by a relative error of at most 0.001.
Values may be sent and summed in bfloat16 or wider, within the bound.
No kernel may reach another device: no remote copies, remote signals or barrier semaphores. Data moves between devices by JAX's collectives and lax.ppermute only.
A program may use at most 32 MiB of HBM per device.

```python
import jax
import jax.numpy as jnp
from jax import lax

BS = 128
PB = 19
BR = 2
BC = 1
SUBS = 4
STEPS = 4
PANEL = 38
CAPM = 6
PCAP = 12
CAP_L = 19
CAP_R = 24
N_PROW = 16
N_PCOL = 64
DEVICES = 1024


def structure(key):
    key = jax.random.fold_in(key, 101)
    keys = jax.random.split(key, 8)
    half_span = SUBS // 2
    full_cols = (CAPM + BC - 1) // BC
    positions = BC * PB
    device = jnp.arange(DEVICES, dtype=jnp.int32)
    row_index = device // N_PCOL
    col_index = device % N_PCOL
    offsets = jnp.arange(STEPS, dtype=jnp.int32) - half_span
    source = row_index[:, None] * N_PCOL + (col_index[:, None] + offsets[None, :]) % N_PCOL
    chosen = jax.random.randint(keys[0], (), 0, DEVICES)
    heavy_panel = jnp.any(device[:, None] == source[chosen][None, :], axis=1)
    column_scores = jax.random.randint(keys[1], (DEVICES, PB), 0, 1 << 20) * PB + jnp.arange(PB, dtype=jnp.int32)[None, :]
    column_ranks = jnp.argsort(jnp.argsort(column_scores, axis=1), axis=1)
    full_blocks = jnp.tile(column_ranks < full_cols, (1, BR))
    block_scores = jax.random.randint(keys[2], (DEVICES, PANEL), 0, 1 << 20) * PANEL + jnp.arange(PANEL, dtype=jnp.int32)[None, :]
    block_scores = jnp.where(heavy_panel[:, None] & full_blocks, block_scores - PANEL * (1 << 20), block_scores)
    filled = jax.random.randint(keys[3], (DEVICES,), CAP_L // 2, CAP_L + 1)
    filled = jnp.where(heavy_panel, CAP_L, filled)
    block_ranks = jnp.argsort(jnp.argsort(block_scores, axis=1), axis=1)
    occupied = (block_ranks < filled[:, None]).astype(jnp.int32)
    slot_scores = jax.random.randint(keys[4], (DEVICES, STEPS, positions), 0, 1 << 20) * positions + jnp.arange(positions, dtype=jnp.int32)[None, None, :]
    usable = jnp.repeat(column_ranks[source] < full_cols, BC, axis=2)
    heavy_device = (device == chosen)[:, None, None]
    slot_scores = jnp.where(heavy_device & usable, slot_scores - positions * (1 << 20), slot_scores)
    slot_keys = jnp.argsort(slot_scores, axis=2)[:, :, :CAPM]
    key_cols = slot_keys // BC
    key_rows = slot_keys % BC
    row_offsets = jnp.arange(BR, dtype=jnp.int32) * PB
    left_index = (key_cols[:, :, :, None] + row_offsets[None, None, None, :]).reshape(DEVICES, STEPS, PCAP)
    right_index = jnp.broadcast_to(jnp.arange(CAPM, dtype=jnp.int32)[None, None, :, None], (DEVICES, STEPS, CAPM, BR)).reshape(DEVICES, STEPS, PCAP)
    out_index = (jnp.arange(BR, dtype=jnp.int32)[None, None, None, :] * BC + key_rows[:, :, :, None]).reshape(DEVICES, STEPS, PCAP)
    occupied_source = occupied[source]
    live = jnp.take_along_axis(occupied_source, left_index, axis=2)
    counts = live.sum(axis=2)
    order = jnp.argsort((1 - live) * PCAP + jnp.arange(PCAP, dtype=jnp.int32)[None, None, :], axis=2)
    left_sorted = jnp.take_along_axis(left_index, order, axis=2)
    right_sorted = jnp.take_along_axis(right_index, order, axis=2)
    out_sorted = jnp.take_along_axis(out_index, order, axis=2)
    listed = jnp.argsort(1 - occupied_source, axis=2, stable=True)
    filled_source = occupied_source.sum(axis=2)
    picks = jax.random.randint(keys[5], (DEVICES, STEPS, PCAP), 0, 1 << 20) % filled_source[:, :, None]
    pad_left = jnp.take_along_axis(listed, picks, axis=2)
    pad_right = jax.random.randint(keys[6], (DEVICES, STEPS, PCAP), 0, CAPM)
    pad_out = jax.random.randint(keys[7], (DEVICES, STEPS, PCAP), 0, BR * BC)
    padding = jnp.arange(PCAP, dtype=jnp.int32)[None, None, :] >= counts[:, :, None]
    lists = jnp.stack([jnp.where(padding, pad_left, left_sorted), jnp.where(padding, pad_right, right_sorted), jnp.where(padding, pad_out, out_sorted)], axis=2)
    return (occupied, lists.astype(jnp.int32), counts.astype(jnp.int32))


def draw_left_mask(key, part):
    return structure(key)[0].reshape(-1)


def draw_pair_lists(key, part):
    return structure(key)[1]


def draw_pair_counts(key, part):
    return structure(key)[2]


def steps_of(own_key, shape, shards, low, high):
    level, own = 1.0, jax.random.fold_in(own_key, 6)
    for dim, shards_of in shards:
        heights = jnp.exp(jax.random.uniform(jax.random.fold_in(own, dim), (shards_of,), jnp.float32, low / len(shards), high / len(shards)))
        level = level * jnp.repeat(heights, shape[dim] // shards_of).reshape([-1 if axis == dim else 1 for axis in range(len(shape))])
    return level


def bell_draw(rng, extent, width, limit, pieces=(), kind=jnp.bfloat16):
    entries = jax.random.normal(rng, extent, jnp.float32) * width
    if len(pieces) > 0:
        entries = steps_of(rng, extent, pieces, -0.22, 0.18) * entries
    return jnp.clip(entries, min=-limit, max=limit).astype(kind)


def setup_inputs(seed: int = 0) -> dict:
    seeds = jax.random.split(jax.random.key(seed), 6)
    return {
        "left_blocks": bell_draw(seeds[0], (DEVICES * PANEL, BS, BS), 1.0, 6.0, ((0, 1024),)),
        "left_mask": draw_left_mask(jax.random.fold_in(seeds[5], 71), 0),
        "right_blocks": bell_draw(seeds[2], (DEVICES * CAP_R, BS, BS), (BS * 16) ** -0.5, 0.125, ((0, 1024),)),
        "pair_lists": draw_pair_lists(jax.random.fold_in(seeds[5], 71), 0),
        "pair_counts": draw_pair_counts(jax.random.fold_in(seeds[5], 71), 0),
    }


def reference(left_blocks, left_mask, right_blocks, pair_lists, pair_counts):
    sub_count = SUBS
    half_span = sub_count // 2
    masked = left_blocks * left_mask.astype(left_blocks.dtype)[:, None, None]
    left_all = masked.reshape(DEVICES, PANEL, BS, BS)
    right_all = right_blocks.reshape(DEVICES, sub_count, CAPM, BS, BS)
    slots = jnp.arange(PCAP, dtype=jnp.int32)
    targets = jnp.arange(BR * BC, dtype=jnp.int32)

    def one_device(device):
        row_index = device // N_PCOL
        col_index = device % N_PCOL
        total = jnp.zeros((BR * BC, BS * BS), jnp.float32)
        for step_index in range(2 * half_span):
            offset = step_index - half_span
            left_source = row_index * N_PCOL + (col_index + offset) % N_PCOL
            row_shift = -1 if offset < 0 else 0
            right_source = ((row_index + row_shift) % N_PROW) * N_PCOL + col_index
            panel_now = left_all[left_source]
            sub_now = right_all[right_source, offset % sub_count]
            step_lists = pair_lists[device, step_index]
            left_taken = panel_now[step_lists[0]].astype(jnp.float32)
            right_taken = sub_now[step_lists[1]].astype(jnp.float32)
            products = jnp.einsum('pij,pjk->pik', left_taken, right_taken, precision=lax.Precision.HIGHEST)
            live_pairs = slots < pair_counts[device, step_index]
            onehot = ((step_lists[2][None, :] == targets[:, None]) & live_pairs[None, :]).astype(jnp.float32)
            total = total + jnp.dot(onehot, products.reshape(PCAP, BS * BS), precision=lax.Precision.HIGHEST, preferred_element_type=jnp.float32)
        return total

    totals = lax.map(one_device, jnp.arange(DEVICES, dtype=jnp.int32))
    grid_blocks = totals.reshape(N_PROW, N_PCOL, BR, BC, BS, BS)
    return grid_blocks.transpose(0, 2, 4, 1, 3, 5).reshape(N_PROW * BR * BS, N_PCOL * BC * BS).astype(jnp.bfloat16)
```

```python
import functools

import jax
import jax.numpy as jnp
from jax import lax
from jax.experimental import pallas as pl
from jax.experimental.pallas import tpu as pltpu
from jax.sharding import PartitionSpec as P

BR = 2
BC = 1
BS = 128
CAP_L = 19
CAPM = 6
META = 16
DEAR = pl.CostEstimate(flops=1 << 36, bytes_accessed=1 << 28, transcendentals=0)
CHEAP = pl.CostEstimate(flops=0, bytes_accessed=1024, transcendentals=0)


def by_pairs(array, pairs):
    return lax.ppermute(array, ("prow", "pcol"), pairs)


def pack_kernel(mask_ref, left_ref, meta_ref, after_ref, packed_ref, sem):
    del after_ref
    panel = left_ref.shape[0]
    tail = pltpu.make_async_copy(meta_ref, packed_ref.at[pl.ds(CAP_L * BS, META)], sem)
    tail.start()
    slot = jnp.int32(0)
    for q in range(panel):
        taken = jnp.logical_and(mask_ref[q] != 0, slot < CAP_L)

        @pl.when(taken)
        def _(q=q, slot=slot):
            row = pl.multiple_of(slot * BS, BS)
            pltpu.make_async_copy(left_ref.at[q], packed_ref.at[pl.ds(row, BS)], sem).start()

        slot = slot + taken.astype(jnp.int32)

    @pl.loop(slot, CAP_L)
    def _(spare):
        row = pl.multiple_of(spare * BS, BS)
        pltpu.make_async_copy(left_ref.at[0], packed_ref.at[pl.ds(row, BS)], sem).start()

    pltpu.make_async_copy(packed_ref, packed_ref, sem).wait()


def pack(left_blocks, left_mask, after):
    meta = jnp.zeros((META, BS), jnp.bfloat16)
    row = jnp.pad(left_mask.astype(jnp.bfloat16), (0, BS - left_mask.shape[0]))
    meta = jnp.broadcast_to(row[None, :], (META, BS))
    return pl.pallas_call(
        pack_kernel,
        out_shape=jax.ShapeDtypeStruct((CAP_L * BS + META, BS), jnp.bfloat16),
        in_specs=[
            pl.BlockSpec(memory_space=pltpu.SMEM),
        ]
        + [pl.BlockSpec(memory_space=pl.ANY)] * 3,
        out_specs=pl.BlockSpec(memory_space=pl.ANY),
        scratch_shapes=[pltpu.SemaphoreType.DMA],
        cost_estimate=CHEAP,
        name="pack_panel",
    )(left_mask, left_blocks, meta, after)


def cut_kernel(first, count, blocks_ref, part_ref, sem):
    copy = pltpu.make_async_copy(blocks_ref.at[pl.ds(first, count)], part_ref, sem)
    copy.start()
    copy.wait()


def cut(blocks, first, count):
    return pl.pallas_call(
        functools.partial(cut_kernel, first, count),
        out_shape=jax.ShapeDtypeStruct((count,) + blocks.shape[1:], blocks.dtype),
        in_specs=[pl.BlockSpec(memory_space=pl.ANY)],
        out_specs=pl.BlockSpec(memory_space=pl.ANY),
        scratch_shapes=[pltpu.SemaphoreType.DMA],
        cost_estimate=CHEAP,
        name="cut_right",
    )(blocks)


def mask_of(packed, panel):
    return packed[CAP_L * BS, :panel].astype(jnp.int32)


def step_kernel(has_acc, lists_ref, count_ref, mask_ref, left_ref, right_ref, *rest):
    if has_acc:
        acc_ref, out_ref, rank_ref, table_ref = rest
    else:
        out_ref, rank_ref, table_ref = rest
    panel = mask_ref.shape[0]
    run = jnp.int32(0)
    for q in range(panel):
        rank_ref[q] = run
        run = run + (mask_ref[q] != 0).astype(jnp.int32)
    for t in range(CAPM * BR):
        table_ref[t] = -1
    for p in range(lists_ref.shape[1]):

        @pl.when(p < count_ref[0])
        def _(p=p):
            at = lists_ref[0, p]
            place = lists_ref[1, p] * BR + lists_ref[2, p]
            table_ref[place] = jnp.where(mask_ref[at] != 0, rank_ref[at], -1)

    for o in range(BR):
        rows = pl.ds(o * BS, BS)
        total = acc_ref[rows, :] if has_acc else jnp.zeros((BS, BS), jnp.float32)
        for m in range(CAPM):
            rank = table_ref[m * BR + o]
            row = pl.multiple_of(jnp.clip(rank, 0, CAP_L - 1) * BS, BS)
            block = left_ref[pl.ds(row, BS), :]
            block = jnp.where(rank >= 0, block, jnp.zeros_like(block))
            total = total + jnp.dot(block, right_ref[m], preferred_element_type=jnp.float32)
        out_ref[rows, :] = total.astype(out_ref.dtype)


def step(lists, count, mask, left, right, acc, dtype, name, cost=CHEAP):
    smem = pl.BlockSpec(memory_space=pltpu.SMEM)
    vmem = pl.BlockSpec(memory_space=pltpu.VMEM)
    args = [lists, count, mask, left, right] + ([] if acc is None else [acc])
    return pl.pallas_call(
        functools.partial(step_kernel, acc is not None),
        out_shape=jax.ShapeDtypeStruct((BR * BS, BS), dtype),
        in_specs=[smem] * 3 + [vmem] * (len(args) - 3),
        out_specs=vmem,
        scratch_shapes=[
            pltpu.SMEM((mask.shape[0],), jnp.int32),
            pltpu.SMEM((CAPM * BR,), jnp.int32),
        ],
        cost_estimate=cost,
        name=name,
    )(*args)


def on_device(n_row, n_col, left_blocks, left_mask, right_blocks, pair_lists, pair_counts):
    panel = left_blocks.shape[0]
    lists, counts = pair_lists[0], pair_counts[0]

    def shift(rows, cols):
        return [
            (r * n_col + c, (r + rows) % n_row * n_col + (c + cols) % n_col)
            for r in range(n_row)
            for c in range(n_col)
        ]

    right = [right_blocks[m * CAPM : (m + 1) * CAPM] for m in range(4)]
    counts_at = [counts[u : u + 1] for u in range(4)]

    first_right = cut(right_blocks, 2 * CAPM, CAPM)
    right_2 = by_pairs(first_right, shift(1, -2))
    packed = pack(left_blocks, left_mask, first_right)
    left_below = by_pairs(packed, shift(0, 1))
    left_above = by_pairs(packed, shift(0, -1))
    ask = jnp.concatenate([lists[0].reshape(-1), counts[:1]])
    asked = by_pairs(ask, shift(0, -2))
    right_3 = by_pairs(right[3], shift(1, 0))

    own = step(lists[2], counts_at[2], left_mask, packed, right[0], None, jnp.float32, "own_step")
    sent = step(
        asked[:36].reshape(3, 12), asked[36:37], left_mask, packed, right_2, None,
        jnp.float32, "partial_for_two_above", DEAR,
    )
    from_two_below = by_pairs(sent, shift(0, 2))
    upper = step(
        lists[3], counts_at[3], mask_of(left_above, panel), left_above, right[1], own,
        jnp.float32, "step_above",
    )
    lower = step(
        lists[1], counts_at[1], mask_of(left_below, panel), left_below, right_3, upper,
        jnp.float32, "step_below",
    )
    return (lower + from_two_below).astype(jnp.bfloat16)


def solution(mesh):
    in_specs = (
        P(("prow", "pcol"), None, None),
        P(("prow", "pcol")),
        P(("prow", "pcol"), None, None),
        P(("prow", "pcol"), None, None, None),
        P(("prow", "pcol"), None),
    )
    return jax.shard_map(
        functools.partial(on_device, mesh.shape["prow"], mesh.shape["pcol"]),
        mesh=mesh,
        in_specs=in_specs,
        out_specs=P("prow", "pcol"),
        check_vma=False,
    )
```

```python
import functools

import jax
import jax.numpy as jnp
from jax import lax
from jax.experimental import pallas as pl
from jax.experimental.pallas import tpu as pltpu
from jax.sharding import PartitionSpec as P

BR = 2
BS = 128
SUBS = 4
CAP_L = 19
CAPM = 6
META = 16
RING = 4
CHEAP = pl.CostEstimate(flops=0, bytes_accessed=1024, transcendentals=0)
SMEM = pl.BlockSpec(memory_space=pltpu.SMEM)
VMEM = pl.BlockSpec(memory_space=pltpu.VMEM)
ANY = pl.BlockSpec(memory_space=pl.ANY)


def by_pairs(array, pairs):
    return lax.ppermute(array, ("prow", "pcol"), pairs)


def cut_kernel(first, blocks_ref, part_ref, sem):
    copy = pltpu.make_async_copy(blocks_ref.at[pl.ds(first, part_ref.shape[0])], part_ref, sem)
    copy.start()
    copy.wait()


def cut(blocks, first, count):
    return pl.pallas_call(
        functools.partial(cut_kernel, first),
        out_shape=jax.ShapeDtypeStruct((count,) + blocks.shape[1:], blocks.dtype),
        in_specs=[ANY],
        out_specs=VMEM,
        scratch_shapes=[pltpu.SemaphoreType.DMA],
        cost_estimate=CHEAP,
        name="cut_right",
    )(blocks)


def pack_kernel(mask_ref, left_ref, after_ref, packed_ref, sem):
    del after_ref
    panel = left_ref.shape[0]
    slot = jnp.int32(0)
    for q in range(panel):
        taken = jnp.logical_and(mask_ref[q] != 0, slot < CAP_L)

        @pl.when(taken)
        def _(q=q, slot=slot):
            row = pl.multiple_of(slot * BS, BS)
            pltpu.make_async_copy(left_ref.at[q], packed_ref.at[pl.ds(row, BS)], sem).start()

        slot = slot + taken.astype(jnp.int32)

    @pl.loop(slot, CAP_L)
    def _(spare):
        row = pl.multiple_of(spare * BS, BS)
        pltpu.make_async_copy(left_ref.at[0], packed_ref.at[pl.ds(row, BS)], sem).start()

    lane = lax.broadcasted_iota(jnp.int32, (META, BS), 1)
    mask = jnp.zeros((META, BS), jnp.float32)
    for q in range(panel):
        mask = jnp.where(lane == q, (mask_ref[q] != 0).astype(jnp.float32), mask)
    packed_ref[pl.ds(CAP_L * BS, META), :] = mask.astype(packed_ref.dtype)
    blocks = packed_ref.at[pl.ds(0, CAP_L * BS)]
    pltpu.make_async_copy(blocks, blocks, sem).wait()


def pack(left_blocks, left_mask, after):
    return pl.pallas_call(
        pack_kernel,
        out_shape=jax.ShapeDtypeStruct((CAP_L * BS + META, BS), jnp.bfloat16),
        in_specs=[SMEM, ANY, ANY],
        out_specs=VMEM,
        scratch_shapes=[pltpu.SemaphoreType.DMA],
        cost_estimate=CHEAP,
        name="pack_panel",
    )(left_mask, left_blocks, after)


def mask_of(packed, panel):
    return packed[CAP_L * BS, :panel].astype(jnp.int32)


def lay_kernel(steps, flag_ref, lists_ref, counts_ref, *refs):
    masks, panels = refs[:2], refs[2 : 2 + 3]
    out_ref, rank_ref, sem = refs[5:]
    out_ref[...] = jnp.zeros_like(out_ref)
    second = flag_ref[0] != 0
    total = jnp.int32(0)
    for at, u in enumerate(steps):
        mask_ref = masks[at]
        run = jnp.int32(0)
        for q in range(mask_ref.shape[0]):
            rank_ref[q] = run
            run = run + (mask_ref[q] != 0).astype(jnp.int32)
        for p in range(lists_ref.shape[3]):
            block = lists_ref[0, u, 0, p]
            slot = lists_ref[0, u, 1, p]
            o = lists_ref[0, u, 2, p]
            live = jnp.logical_and(p < counts_ref[0, u], mask_ref[block] != 0)
            row = pl.multiple_of(jnp.minimum(rank_ref[block], CAP_L - 1) * BS, BS)
            down = pl.multiple_of(o * BS, BS)
            along = pl.multiple_of((at * CAPM + slot) * BS, BS)
            target = out_ref.at[pl.ds(down, BS), pl.ds(along, BS)]

            def fetch(panel_ref):
                pltpu.make_async_copy(panel_ref.at[pl.ds(row, BS)], target, sem).start()

            if at == 0:
                pl.when(live)(lambda: fetch(panels[0]))
            else:
                pl.when(jnp.logical_and(live, jnp.logical_not(second)))(lambda: fetch(panels[1]))
                pl.when(jnp.logical_and(live, second))(lambda: fetch(panels[2]))
            total = total + live.astype(jnp.int32)

    @pl.loop(0, total)
    def _(_):
        one = panels[0].at[pl.ds(0, BS)]
        pltpu.make_async_copy(one, out_ref.at[pl.ds(0, BS), pl.ds(0, BS)], sem).wait()


def lay(steps, flag, lists, counts, masks, panels, name):
    return pl.pallas_call(
        functools.partial(lay_kernel, steps),
        out_shape=jax.ShapeDtypeStruct((BR * BS, 2 * CAPM * BS), jnp.bfloat16),
        in_specs=[SMEM] * 5 + [ANY] * 3,
        out_specs=VMEM,
        scratch_shapes=[pltpu.SMEM((masks[0].shape[0],), jnp.int32), pltpu.SemaphoreType.DMA],
        cost_estimate=CHEAP,
        name=name,
    )(flag, lists, counts, *masks, *panels)


def on_device(n_row, n_col, left_blocks, left_mask, right_blocks, pair_lists, pair_counts):
    panel = left_blocks.shape[0]

    def shift(rows, cols, places=range(RING)):
        return [
            (r * n_col + c, (r + rows) % n_row * n_col + (c + cols) % n_col)
            for r in range(n_row)
            for c in range(n_col)
            if c % RING in places
        ]

    half = 2 * CAPM
    sent_right = cut(right_blocks, half, half)
    right_before = by_pairs(sent_right, shift(1, 0))
    packed = pack(left_blocks, left_mask, sent_right)
    two_below = by_pairs(packed, shift(0, 2))
    one_below = by_pairs(packed, shift(0, 1, range(RING - 1)))
    one_above = by_pairs(packed, shift(0, -1))
    handed = by_pairs(two_below, shift(0, -1, [1]))

    first = (lax.axis_index("pcol") % RING == 0).astype(jnp.int32).reshape(1)
    never = jnp.zeros((1,), jnp.int32)
    upper_left = lay(
        (2, 3), never, pair_lists, pair_counts,
        [left_mask, mask_of(one_above, panel)],
        [packed, one_above, one_above], "lay_upper",
    )
    mask_below = jnp.where(first != 0, mask_of(handed, panel), mask_of(one_below, panel))
    lower_left = lay(
        (0, 1), first, pair_lists, pair_counts,
        [mask_of(two_below, panel), mask_below],
        [two_below, one_below, handed], "lay_lower",
    )

    def times(left, right):
        return jnp.dot(left, right.reshape(half * BS, BS), preferred_element_type=jnp.float32)

    total = times(upper_left, right_blocks[:half]) + times(lower_left, right_before)
    return total.astype(jnp.bfloat16)


def solution(mesh):
    in_specs = (
        P(("prow", "pcol"), None, None),
        P(("prow", "pcol")),
        P(("prow", "pcol"), None, None),
        P(("prow", "pcol"), None, None, None),
        P(("prow", "pcol"), None),
    )
    return jax.shard_map(
        functools.partial(on_device, mesh.shape["prow"], mesh.shape["pcol"]),
        mesh=mesh,
        in_specs=in_specs,
        out_specs=P("prow", "pcol"),
        check_vma=False,
    )
```

```python
import functools

import jax
import jax.numpy as jnp
from jax import lax
from jax.experimental import pallas as pl
from jax.experimental.pallas import tpu as pltpu
from jax.sharding import PartitionSpec as P

BR = 2
BS = 128
SUBS = 4
CAP_L = 19
CAPM = 6
META = 16
RING = 4
CHEAP = pl.CostEstimate(flops=0, bytes_accessed=1024, transcendentals=0)
SMEM = pl.BlockSpec(memory_space=pltpu.SMEM)
VMEM = pl.BlockSpec(memory_space=pltpu.VMEM)
ANY = pl.BlockSpec(memory_space=pl.ANY)


def by_pairs(array, pairs):
    return lax.ppermute(array, ("prow", "pcol"), pairs)


def stage_kernel(mask_ref, left_ref, right_ref, packed_ref, part_ref, sem, part_sem):
    panel = left_ref.shape[0]
    half = part_ref.shape[0]
    part = pltpu.make_async_copy(right_ref.at[pl.ds(half, half)], part_ref, part_sem)
    part.start()
    slot = jnp.int32(0)
    for q in range(panel):
        taken = jnp.logical_and(mask_ref[q] != 0, slot < CAP_L)

        @pl.when(taken)
        def _(q=q, slot=slot):
            row = pl.multiple_of(slot * BS, BS)
            pltpu.make_async_copy(left_ref.at[q], packed_ref.at[pl.ds(row, BS)], sem).start()

        slot = slot + taken.astype(jnp.int32)

    @pl.loop(slot, CAP_L)
    def _(spare):
        row = pl.multiple_of(spare * BS, BS)
        pltpu.make_async_copy(left_ref.at[0], packed_ref.at[pl.ds(row, BS)], sem).start()

    lane = lax.broadcasted_iota(jnp.int32, (META, BS), 1)
    mask = jnp.zeros((META, BS), jnp.float32)
    for q in range(panel):
        mask = jnp.where(lane == q, (mask_ref[q] != 0).astype(jnp.float32), mask)
    packed_ref[pl.ds(CAP_L * BS, META), :] = mask.astype(packed_ref.dtype)
    blocks = packed_ref.at[pl.ds(0, CAP_L * BS)]
    pltpu.make_async_copy(blocks, blocks, sem).wait()
    part.wait()


def stage(left_mask, left_blocks, right_blocks):
    return pl.pallas_call(
        stage_kernel,
        out_shape=[
            jax.ShapeDtypeStruct((CAP_L * BS + META, BS), jnp.bfloat16),
            jax.ShapeDtypeStruct((2 * CAPM, BS, BS), jnp.bfloat16),
        ],
        in_specs=[SMEM, ANY, ANY],
        out_specs=[VMEM, VMEM],
        scratch_shapes=[pltpu.SemaphoreType.DMA, pltpu.SemaphoreType.DMA],
        cost_estimate=CHEAP,
        name="pack_and_cut",
    )(left_mask, left_blocks, right_blocks)


def mask_of(packed, panel):
    return packed[CAP_L * BS, :panel].astype(jnp.int32)


def lay_kernel(steps, lists_ref, counts_ref, *refs):
    masks, panels = refs[: len(steps)], refs[len(steps) : -3]
    out_ref, rank_ref, sem = refs[-3:]
    out_ref[...] = jnp.zeros_like(out_ref)
    column = lax.axis_index("pcol")
    total = jnp.int32(0)
    for at, (u, sources) in enumerate(steps):
        mask_ref = masks[at]
        run = jnp.int32(0)
        for q in range(mask_ref.shape[0]):
            rank_ref[q] = run
            run = run + (mask_ref[q] != 0).astype(jnp.int32)
        held = [(panels[i], where(column)) for i, where in sources]
        for p in range(lists_ref.shape[3]):
            block = lists_ref[0, u, 0, p]
            slot = lists_ref[0, u, 1, p]
            o = lists_ref[0, u, 2, p]
            live = jnp.logical_and(p < counts_ref[0, u], mask_ref[block] != 0)
            row = pl.multiple_of(jnp.minimum(rank_ref[block], CAP_L - 1) * BS, BS)
            down = pl.multiple_of(o * BS, BS)
            along = pl.multiple_of((at * CAPM + slot) * BS, BS)
            target = out_ref.at[pl.ds(down, BS), pl.ds(along, BS)]
            for panel_ref, here in held:
                taken = jnp.logical_and(live, here)

                @pl.when(taken)
                def _(panel_ref=panel_ref, row=row, target=target):
                    pltpu.make_async_copy(panel_ref.at[pl.ds(row, BS)], target, sem).start()

                total = total + taken.astype(jnp.int32)

    @pl.loop(0, total)
    def _(_):
        one = panels[0].at[pl.ds(0, BS)]
        pltpu.make_async_copy(one, out_ref.at[pl.ds(0, BS), pl.ds(0, BS)], sem).wait()


def lay(steps, lists, counts, masks, panels, name):
    return pl.pallas_call(
        functools.partial(lay_kernel, steps),
        out_shape=jax.ShapeDtypeStruct((BR * BS, len(steps) * CAPM * BS), jnp.bfloat16),
        in_specs=[SMEM] * (2 + len(masks)) + [ANY] * len(panels),
        out_specs=VMEM,
        scratch_shapes=[pltpu.SMEM((masks[0].shape[0],), jnp.int32), pltpu.SemaphoreType.DMA],
        cost_estimate=CHEAP,
        name=name,
    )(lists, counts, *masks, *panels)


def finish_kernel(steps, lists_ref, counts_ref, *refs):
    masks, panels, rights = refs[:2], refs[2:4], refs[4:6]
    known_ref, new_ref, out_ref, left_ref, right_ref, total_ref, rank_ref, sems = refs[6:]
    column = lax.axis_index("pcol")
    total_ref[...] = known_ref[...] + new_ref[...]
    for u, which, (side, first), here in steps:

        @pl.when(here(column))
        def _(u=u, which=which, side=side, first=first):
            part = rights[side].at[pl.ds(first * CAPM, CAPM)]
            fetch_right = pltpu.make_async_copy(part, right_ref, sems.at[0])
            fetch_right.start()
            left_ref[...] = jnp.zeros_like(left_ref)
            run = jnp.int32(0)
            for q in range(masks[which].shape[0]):
                rank_ref[q] = run
                run = run + (masks[which][q] != 0).astype(jnp.int32)
            count = jnp.int32(0)
            for p in range(lists_ref.shape[3]):
                block = lists_ref[0, u, 0, p]
                live = jnp.logical_and(p < counts_ref[0, u], masks[which][block] != 0)
                row = pl.multiple_of(jnp.minimum(rank_ref[block], CAP_L - 1) * BS, BS)
                along = pl.multiple_of(lists_ref[0, u, 1, p] * BS, BS)
                down = pl.multiple_of(lists_ref[0, u, 2, p] * BS, BS)

                @pl.when(live)
                def _(row=row, down=down, along=along):
                    target = left_ref.at[pl.ds(down, BS), pl.ds(along, BS)]
                    source = panels[which].at[pl.ds(row, BS)]
                    pltpu.make_async_copy(source, target, sems.at[1]).start()

                count = count + live.astype(jnp.int32)

            @pl.loop(0, count)
            def _(_):
                one = panels[which].at[pl.ds(0, BS)]
                target = left_ref.at[pl.ds(0, BS), pl.ds(0, BS)]
                pltpu.make_async_copy(one, target, sems.at[1]).wait()

            fetch_right.wait()
            for m in range(CAPM):
                total_ref[...] += jnp.dot(
                    left_ref[:, m * BS : (m + 1) * BS],
                    right_ref[m],
                    preferred_element_type=jnp.float32,
                )

    out_ref[...] = total_ref[...].astype(out_ref.dtype)


def finish(steps, lists, counts, masks, panels, rights, known, new):
    return pl.pallas_call(
        functools.partial(finish_kernel, steps),
        out_shape=jax.ShapeDtypeStruct(new.shape, jnp.bfloat16),
        in_specs=[SMEM] * 4 + [ANY] * 4 + [VMEM] * 2,
        out_specs=VMEM,
        scratch_shapes=[
            pltpu.VMEM((BR * BS, CAPM * BS), jnp.bfloat16),
            pltpu.VMEM((CAPM, BS, BS), jnp.bfloat16),
            pltpu.VMEM(new.shape, jnp.float32),
            pltpu.SMEM((masks[0].shape[0],), jnp.int32),
            pltpu.SemaphoreType.DMA((2,)),
        ],
        cost_estimate=CHEAP,
        name="finish",
    )(lists, counts, *masks, *panels, *rights, known, new)


def on_device(n_row, n_col, left_blocks, left_mask, right_blocks, pair_lists, pair_counts):
    panel = left_blocks.shape[0]
    last = n_col - 1
    half = 2 * CAPM

    def shift(rows, cols, chosen):
        return [
            (r * n_col + c, (r + rows) % n_row * n_col + (c + cols) % n_col)
            for r in range(n_row)
            for c in range(n_col)
            if chosen(c)
        ]

    packed, sent_right = stage(left_mask, left_blocks, right_blocks)
    two_below = by_pairs(packed, shift(0, 2, lambda c: c < last - 1))
    one_above = by_pairs(packed, shift(0, -1, lambda c: c > 0))
    one_below = by_pairs(packed, shift(0, 1, lambda c: c % RING < RING - 1))
    right_before = by_pairs(sent_right, shift(1, 0, lambda c: True))
    column = lax.axis_index("pcol")
    passed = jnp.where(jnp.logical_or(column % RING == 1, column == 2), two_below, packed)
    handed = by_pairs(
        passed,
        shift(0, -1, lambda c: c % RING == 1 and c != 1)
        + shift(0, 2, lambda c: c >= last - 1)
        + shift(0, -3, lambda c: c == 2),
    )
    around = by_pairs(passed, shift(0, 1, lambda c: c == last))

    laid = lay(
        (
            (0, ((0, lambda c: c >= 2),)),
            (1, ((1, lambda c: lax.rem(c, RING) != 0),)),
            (2, ((2, lambda c: c >= 0),)),
            (3, ((3, lambda c: c < last),)),
        ),
        pair_lists, pair_counts,
        [mask_of(two_below, panel), mask_of(one_below, panel), left_mask, mask_of(one_above, panel)],
        [two_below, one_below, packed, one_above], "lay_left",
    )

    def times(left, right):
        return jnp.dot(left, right.reshape(half * BS, BS), preferred_element_type=jnp.float32)

    known = times(laid[:, half * BS :], right_blocks[:half])
    new = times(laid[:, : half * BS], right_before)
    return finish(
        (
            (0, 1, (0, 0), lambda c: c < 2),
            (1, 1, (0, 1), lambda c: jnp.logical_and(lax.rem(c, RING) == 0, c != 0)),
            (1, 0, (0, 1), lambda c: c == 0),
            (3, 1, (1, 1), lambda c: c == last),
        ),
        pair_lists, pair_counts,
        [mask_of(around, panel), mask_of(handed, panel)],
        [around, handed], [right_before, right_blocks], known, new,
    )


def solution(mesh):
    in_specs = (
        P(("prow", "pcol"), None, None),
        P(("prow", "pcol")),
        P(("prow", "pcol"), None, None),
        P(("prow", "pcol"), None, None, None),
        P(("prow", "pcol"), None),
    )
    return jax.shard_map(
        functools.partial(on_device, mesh.shape["prow"], mesh.shape["pcol"]),
        mesh=mesh,
        in_specs=in_specs,
        out_specs=P("prow", "pcol"),
        check_vma=False,
    )
```

```python
import functools

import jax
import jax.numpy as jnp
from jax import lax
from jax.experimental import pallas as pl
from jax.experimental.pallas import tpu as pltpu
from jax.sharding import PartitionSpec as P

BR = 2
BS = 128
SUBS = 4
CAP_L = 19
CAPM = 6
META = 16
RING = 4
CHEAP = pl.CostEstimate(flops=0, bytes_accessed=1024, transcendentals=0)
DEAR = pl.CostEstimate(flops=1 << 35, bytes_accessed=1 << 20, transcendentals=0)
ROOM = pltpu.CompilerParams(vmem_limit_bytes=16 << 20)
SMEM = pl.BlockSpec(memory_space=pltpu.SMEM)
VMEM = pl.BlockSpec(memory_space=pltpu.VMEM)
ANY = pl.BlockSpec(memory_space=pl.ANY)


def by_pairs(array, pairs):
    return lax.ppermute(array, ("prow", "pcol"), pairs)


def stage_kernel(mask_ref, left_ref, right_ref, packed_ref, part_ref, sem, part_sem):
    panel = left_ref.shape[0]
    half = part_ref.shape[0]
    part = pltpu.make_async_copy(right_ref.at[pl.ds(half, half)], part_ref, part_sem)
    part.start()
    slot = jnp.int32(0)
    for q in range(panel):
        taken = jnp.logical_and(mask_ref[q] != 0, slot < CAP_L)

        @pl.when(taken)
        def _(q=q, slot=slot):
            row = pl.multiple_of(slot * BS, BS)
            pltpu.make_async_copy(left_ref.at[q], packed_ref.at[pl.ds(row, BS)], sem).start()

        slot = slot + taken.astype(jnp.int32)

    @pl.loop(slot, CAP_L)
    def _(spare):
        row = pl.multiple_of(spare * BS, BS)
        pltpu.make_async_copy(left_ref.at[0], packed_ref.at[pl.ds(row, BS)], sem).start()

    lane = lax.broadcasted_iota(jnp.int32, (META, BS), 1)
    mask = jnp.zeros((META, BS), jnp.float32)
    for q in range(panel):
        mask = jnp.where(lane == q, (mask_ref[q] != 0).astype(jnp.float32), mask)
    packed_ref[pl.ds(CAP_L * BS, META), :] = mask.astype(packed_ref.dtype)
    blocks = packed_ref.at[pl.ds(0, CAP_L * BS)]
    pltpu.make_async_copy(blocks, blocks, sem).wait()
    part.wait()


def stage(left_mask, left_blocks, right_blocks):
    return pl.pallas_call(
        stage_kernel,
        out_shape=[
            jax.ShapeDtypeStruct((CAP_L * BS + META, BS), jnp.bfloat16),
            jax.ShapeDtypeStruct((2 * CAPM, BS, BS), jnp.bfloat16),
        ],
        in_specs=[SMEM, ANY, ANY],
        out_specs=[VMEM, VMEM],
        scratch_shapes=[pltpu.SemaphoreType.DMA, pltpu.SemaphoreType.DMA],
        compiler_params=ROOM,
        cost_estimate=CHEAP,
        name="pack_and_cut",
    )(left_mask, left_blocks, right_blocks)


def mask_of(packed, panel):
    return packed[CAP_L * BS, :panel].astype(jnp.int32)


def place(u, at, lists_ref, counts_ref, mask_ref, sources, into_ref, rank_ref, sem):
    column = lax.axis_index("pcol")
    run = jnp.int32(0)
    for q in range(mask_ref.shape[0]):
        rank_ref[q] = run
        run = run + (mask_ref[q] != 0).astype(jnp.int32)
    held = [(panel_ref, where(column)) for panel_ref, where in sources]
    total = jnp.int32(0)
    for p in range(lists_ref.shape[3]):
        block = lists_ref[0, u, 0, p]
        slot = lists_ref[0, u, 1, p]
        o = lists_ref[0, u, 2, p]
        live = jnp.logical_and(p < counts_ref[0, u], mask_ref[block] != 0)
        row = pl.multiple_of(jnp.minimum(rank_ref[block], CAP_L - 1) * BS, BS)
        down = pl.multiple_of(o * BS, BS)
        along = pl.multiple_of((at * CAPM + slot) * BS, BS)
        target = into_ref.at[pl.ds(down, BS), pl.ds(along, BS)]
        for panel_ref, here in held:
            taken = jnp.logical_and(live, here)

            @pl.when(taken)
            def _(panel_ref=panel_ref, row=row, target=target):
                pltpu.make_async_copy(panel_ref.at[pl.ds(row, BS)], target, sem).start()

            total = total + taken.astype(jnp.int32)
    return total


def drain(total, panel_ref, into_ref, sem):
    @pl.loop(0, total)
    def _(_):
        one = panel_ref.at[pl.ds(0, BS)]
        pltpu.make_async_copy(one, into_ref.at[pl.ds(0, BS), pl.ds(0, BS)], sem).wait()


def multiply(left_ref, right_ref, total_ref):
    for m in range(right_ref.shape[0]):
        total_ref[...] += jnp.dot(
            left_ref[:, m * BS : (m + 1) * BS], right_ref[m], preferred_element_type=jnp.float32
        )


def early_kernel(
    last, lists_ref, counts_ref, own_mask_ref, mask_ref, own_ref, above_ref, right_ref,
    known_ref, left_ref, held_ref, rank_ref, sem, right_sem,
):
    fetch_right = pltpu.make_async_copy(
        right_ref.at[pl.ds(0, held_ref.shape[0])], held_ref, right_sem
    )
    fetch_right.start()
    left_ref[...] = jnp.zeros_like(left_ref)
    own = ((own_ref, lambda c: c >= 0),)
    above = ((above_ref, lambda c: c < last),)
    total = place(2, 0, lists_ref, counts_ref, own_mask_ref, own, left_ref, rank_ref, sem)
    total += place(3, 1, lists_ref, counts_ref, mask_ref, above, left_ref, rank_ref, sem)
    drain(total, own_ref, left_ref, sem)
    fetch_right.wait()
    known_ref[...] = jnp.zeros_like(known_ref)
    multiply(left_ref, held_ref, known_ref)


def early(last, lists, counts, masks, panels, right):
    half = 2 * CAPM
    return pl.pallas_call(
        functools.partial(early_kernel, last),
        out_shape=jax.ShapeDtypeStruct((BR * BS, BS), jnp.float32),
        in_specs=[SMEM] * 4 + [ANY] * 3,
        out_specs=VMEM,
        scratch_shapes=[
            pltpu.VMEM((BR * BS, half * BS), jnp.bfloat16),
            pltpu.VMEM((half, BS, BS), jnp.bfloat16),
            pltpu.SMEM((masks[0].shape[0],), jnp.int32),
            pltpu.SemaphoreType.DMA,
            pltpu.SemaphoreType.DMA,
        ],
        compiler_params=ROOM,
        cost_estimate=DEAR,
        name="own_and_above",
    )(lists, counts, *masks, *panels, right)


def late_kernel(
    last, lists_ref, counts_ref, two_mask_ref, one_mask_ref, handed_mask_ref,
    two_ref, one_ref, handed_ref, right_ref, early_ref,
    laid_ref, known_ref, left_ref, held_ref, rank_ref, sem, right_sem,
):
    laid_ref[...] = jnp.zeros_like(laid_ref)
    two = ((two_ref, lambda c: c >= 0),)
    one = (
        (one_ref, lambda c: lax.rem(c, RING) != 0),
        (handed_ref, lambda c: lax.rem(c, RING) == 0),
    )
    total = place(0, 0, lists_ref, counts_ref, two_mask_ref, two, laid_ref, rank_ref, sem)
    total += place(1, 1, lists_ref, counts_ref, one_mask_ref, one, laid_ref, rank_ref, sem)
    known_ref[...] = early_ref[...]
    drain(total, two_ref, laid_ref, sem)

    @pl.when(lax.axis_index("pcol") == last)
    def _():
        fetch_right = pltpu.make_async_copy(
            right_ref.at[pl.ds(CAPM, CAPM)], held_ref, right_sem
        )
        fetch_right.start()
        left_ref[...] = jnp.zeros_like(left_ref)
        above = ((handed_ref, lambda c: c >= 0),)
        count = place(
            3, 0, lists_ref, counts_ref, handed_mask_ref, above, left_ref, rank_ref, sem
        )
        drain(count, handed_ref, left_ref, sem)
        fetch_right.wait()
        multiply(left_ref, held_ref, known_ref)


def late(last, lists, counts, masks, panels, right, known):
    return pl.pallas_call(
        functools.partial(late_kernel, last),
        out_shape=[
            jax.ShapeDtypeStruct((BR * BS, 2 * CAPM * BS), jnp.bfloat16),
            jax.ShapeDtypeStruct((BR * BS, BS), jnp.float32),
        ],
        in_specs=[SMEM] * 5 + [ANY] * 4 + [VMEM],
        out_specs=[VMEM, VMEM],
        scratch_shapes=[
            pltpu.VMEM((BR * BS, CAPM * BS), jnp.bfloat16),
            pltpu.VMEM((CAPM, BS, BS), jnp.bfloat16),
            pltpu.SMEM((masks[0].shape[0],), jnp.int32),
            pltpu.SemaphoreType.DMA,
            pltpu.SemaphoreType.DMA,
        ],
        compiler_params=ROOM,
        cost_estimate=CHEAP,
        name="lay_below",
    )(lists, counts, *masks, *panels, right, known)


def last_kernel(left_ref, right_ref, known_ref, out_ref):
    new = jnp.dot(left_ref[...], right_ref[...], preferred_element_type=jnp.float32)
    out_ref[...] = (known_ref[...] + new).astype(out_ref.dtype)


def last_product(left, right, known):
    return pl.pallas_call(
        last_kernel,
        out_shape=jax.ShapeDtypeStruct(known.shape, jnp.bfloat16),
        in_specs=[VMEM] * 3,
        out_specs=VMEM,
        compiler_params=ROOM,
        cost_estimate=CHEAP,
        name="last_product",
    )(left, right, known)


def on_device(n_row, n_col, left_blocks, left_mask, right_blocks, pair_lists, pair_counts):
    panel = left_blocks.shape[0]
    last = n_col - 1
    half = 2 * CAPM

    def shift(rows, cols, chosen):
        return [
            (r * n_col + c, (r + rows) % n_row * n_col + (c + cols) % n_col)
            for r in range(n_row)
            for c in range(n_col)
            if chosen(c)
        ]

    packed, sent_right = stage(left_mask, left_blocks, right_blocks)
    two_below = by_pairs(packed, shift(0, 2, lambda c: True))
    one_above = by_pairs(packed, shift(0, -1, lambda c: c > 0))
    one_below = by_pairs(packed, shift(0, 1, lambda c: c % RING < RING - 1))
    right_before = by_pairs(sent_right, shift(1, 0, lambda c: True))
    handed = by_pairs(
        two_below,
        shift(0, -1, lambda c: c % RING == 1) + shift(0, -3, lambda c: c == 2),
    )

    column = lax.axis_index("pcol")
    mask_handed = mask_of(handed, panel)
    known = early(
        last, pair_lists, pair_counts, [left_mask, mask_of(one_above, panel)],
        [packed, one_above], right_blocks,
    )
    mask_one = jnp.where(column % RING == 0, mask_handed, mask_of(one_below, panel))
    laid, known = late(
        last, pair_lists, pair_counts, [mask_of(two_below, panel), mask_one, mask_handed],
        [two_below, one_below, handed], right_blocks, known,
    )
    return last_product(laid, right_before.reshape(half * BS, BS), known)


def solution(mesh):
    in_specs = (
        P(("prow", "pcol"), None, None),
        P(("prow", "pcol")),
        P(("prow", "pcol"), None, None),
        P(("prow", "pcol"), None, None, None),
        P(("prow", "pcol"), None),
    )
    return jax.shard_map(
        functools.partial(on_device, mesh.shape["prow"], mesh.shape["pcol"]),
        mesh=mesh,
        in_specs=in_specs,
        out_specs=P("prow", "pcol"),
        check_vma=False,
    )
```

```python
import functools

import jax
import jax.numpy as jnp
from jax import lax
from jax.experimental import pallas as pl
from jax.experimental.pallas import tpu as pltpu
from jax.sharding import PartitionSpec as P

BR = 2
BS = 128
SUBS = 4
CAP_L = 19
CAPM = 6
META = 16
RING = 4
CHEAP = pl.CostEstimate(flops=0, bytes_accessed=1024, transcendentals=0)
DEAR = pl.CostEstimate(flops=1 << 35, bytes_accessed=1 << 20, transcendentals=0)
ROOM = pltpu.CompilerParams(vmem_limit_bytes=16 << 20)
SMEM = pl.BlockSpec(memory_space=pltpu.SMEM)
VMEM = pl.BlockSpec(memory_space=pltpu.VMEM)
ANY = pl.BlockSpec(memory_space=pl.ANY)


def by_pairs(array, pairs):
    return lax.ppermute(array, ("prow", "pcol"), pairs)


def stage_kernel(mask_ref, left_ref, right_ref, packed_ref, part_ref, sem, part_sem):
    panel = left_ref.shape[0]
    half = part_ref.shape[0]
    part = pltpu.make_async_copy(right_ref.at[pl.ds(half, half)], part_ref, part_sem)
    part.start()
    slot = jnp.int32(0)
    for q in range(panel):
        taken = jnp.logical_and(mask_ref[q] != 0, slot < CAP_L)

        @pl.when(taken)
        def _(q=q, slot=slot):
            row = pl.multiple_of(slot * BS, BS)
            pltpu.make_async_copy(left_ref.at[q], packed_ref.at[pl.ds(row, BS)], sem).start()

        slot = slot + taken.astype(jnp.int32)

    @pl.loop(slot, CAP_L)
    def _(spare):
        row = pl.multiple_of(spare * BS, BS)
        pltpu.make_async_copy(left_ref.at[0], packed_ref.at[pl.ds(row, BS)], sem).start()

    lane = lax.broadcasted_iota(jnp.int32, (META, BS), 1)
    mask = jnp.zeros((META, BS), jnp.float32)
    for q in range(panel):
        mask = jnp.where(lane == q, (mask_ref[q] != 0).astype(jnp.float32), mask)
    packed_ref[pl.ds(CAP_L * BS, META), :] = mask.astype(packed_ref.dtype)
    blocks = packed_ref.at[pl.ds(0, CAP_L * BS)]
    pltpu.make_async_copy(blocks, blocks, sem).wait()
    part.wait()


def stage(left_mask, left_blocks, right_blocks):
    return pl.pallas_call(
        stage_kernel,
        out_shape=[
            jax.ShapeDtypeStruct((CAP_L * BS + META, BS), jnp.bfloat16),
            jax.ShapeDtypeStruct((2 * CAPM, BS, BS), jnp.bfloat16),
        ],
        in_specs=[SMEM, ANY, ANY],
        out_specs=[VMEM, VMEM],
        scratch_shapes=[pltpu.SemaphoreType.DMA, pltpu.SemaphoreType.DMA],
        compiler_params=pltpu.CompilerParams(vmem_limit_bytes=62 << 20),
        cost_estimate=CHEAP,
        name="pack_and_cut",
    )(left_mask, left_blocks, right_blocks)


def mask_of(packed, panel):
    return packed[CAP_L * BS, :panel].astype(jnp.int32)


def place(u, at, lists_ref, counts_ref, mask_ref, sources, into_ref, rank_ref, sem):
    column = lax.axis_index("pcol")
    run = jnp.int32(0)
    for q in range(mask_ref.shape[0]):
        rank_ref[q] = run
        run = run + (mask_ref[q] != 0).astype(jnp.int32)
    held = [(panel_ref, where(column)) for panel_ref, where in sources]
    total = jnp.int32(0)
    for p in range(lists_ref.shape[3]):
        block = lists_ref[0, u, 0, p]
        slot = lists_ref[0, u, 1, p]
        o = lists_ref[0, u, 2, p]
        live = jnp.logical_and(p < counts_ref[0, u], mask_ref[block] != 0)
        row = pl.multiple_of(jnp.minimum(rank_ref[block], CAP_L - 1) * BS, BS)
        down = pl.multiple_of(o * BS, BS)
        along = pl.multiple_of((at * CAPM + slot) * BS, BS)
        target = into_ref.at[pl.ds(down, BS), pl.ds(along, BS)]
        for panel_ref, here in held:
            taken = jnp.logical_and(live, here)

            @pl.when(taken)
            def _(panel_ref=panel_ref, row=row, target=target):
                pltpu.make_async_copy(panel_ref.at[pl.ds(row, BS)], target, sem).start()

            total = total + taken.astype(jnp.int32)
    return total


def drain(total, panel_ref, into_ref, sem):
    @pl.loop(0, total)
    def _(_):
        one = panel_ref.at[pl.ds(0, BS)]
        pltpu.make_async_copy(one, into_ref.at[pl.ds(0, BS), pl.ds(0, BS)], sem).wait()


def multiply(left_ref, right_ref, total_ref):
    for m in range(right_ref.shape[0]):
        total_ref[...] += jnp.dot(
            left_ref[:, m * BS : (m + 1) * BS], right_ref[m], preferred_element_type=jnp.float32
        )


def one_kernel(
    u, here, lists_ref, counts_ref, mask_ref, panel_ref, right_ref, *refs,
):
    before_ref = refs[0] if len(refs) == 7 else None
    known_ref, left_ref, held_ref, rank_ref, sem, right_sem = refs[-6:]
    fetch_right = pltpu.make_async_copy(
        right_ref.at[pl.ds((u - 2) * CAPM, CAPM)], held_ref, right_sem
    )
    fetch_right.start()
    left_ref[...] = jnp.zeros_like(left_ref)
    source = ((panel_ref, here),)
    total = place(u, 0, lists_ref, counts_ref, mask_ref, source, left_ref, rank_ref, sem)
    drain(total, panel_ref, left_ref, sem)
    fetch_right.wait()
    known_ref[...] = jnp.zeros_like(known_ref) if before_ref is None else before_ref[...]
    multiply(left_ref, held_ref, known_ref)


def one_step(u, here, lists, counts, mask, panel, right, before, cost, name):
    more = [] if before is None else [before]
    return pl.pallas_call(
        functools.partial(one_kernel, u, here),
        out_shape=jax.ShapeDtypeStruct((BR * BS, BS), jnp.float32),
        in_specs=[SMEM] * 3 + [ANY] * 2 + [VMEM] * len(more),
        out_specs=VMEM,
        scratch_shapes=[
            pltpu.VMEM((BR * BS, CAPM * BS), jnp.bfloat16),
            pltpu.VMEM((CAPM, BS, BS), jnp.bfloat16),
            pltpu.SMEM((mask.shape[0],), jnp.int32),
            pltpu.SemaphoreType.DMA,
            pltpu.SemaphoreType.DMA,
        ],
        compiler_params=ROOM,
        cost_estimate=cost,
        name=name,
    )(lists, counts, mask, panel, right, *more)


def late_kernel(
    last, lists_ref, counts_ref, two_mask_ref, one_mask_ref, handed_mask_ref,
    two_ref, one_ref, handed_ref, right_ref, early_ref,
    laid_ref, known_ref, left_ref, held_ref, rank_ref, sem, right_sem,
):
    laid_ref[...] = jnp.zeros_like(laid_ref)
    two = ((two_ref, lambda c: c >= 0),)
    one = (
        (one_ref, lambda c: lax.rem(c, RING) != 0),
        (handed_ref, lambda c: lax.rem(c, RING) == 0),
    )
    total = place(0, 0, lists_ref, counts_ref, two_mask_ref, two, laid_ref, rank_ref, sem)
    total += place(1, 1, lists_ref, counts_ref, one_mask_ref, one, laid_ref, rank_ref, sem)
    known_ref[...] = early_ref[...]
    drain(total, two_ref, laid_ref, sem)

    @pl.when(lax.axis_index("pcol") == last)
    def _():
        fetch_right = pltpu.make_async_copy(
            right_ref.at[pl.ds(CAPM, CAPM)], held_ref, right_sem
        )
        fetch_right.start()
        left_ref[...] = jnp.zeros_like(left_ref)
        above = ((handed_ref, lambda c: c >= 0),)
        count = place(
            3, 0, lists_ref, counts_ref, handed_mask_ref, above, left_ref, rank_ref, sem
        )
        drain(count, handed_ref, left_ref, sem)
        fetch_right.wait()
        multiply(left_ref, held_ref, known_ref)


def late(last, lists, counts, masks, panels, right, known):
    return pl.pallas_call(
        functools.partial(late_kernel, last),
        out_shape=[
            jax.ShapeDtypeStruct((BR * BS, 2 * CAPM * BS), jnp.bfloat16),
            jax.ShapeDtypeStruct((BR * BS, BS), jnp.float32),
        ],
        in_specs=[SMEM] * 5 + [ANY] * 4 + [VMEM],
        out_specs=[VMEM, VMEM],
        scratch_shapes=[
            pltpu.VMEM((BR * BS, CAPM * BS), jnp.bfloat16),
            pltpu.VMEM((CAPM, BS, BS), jnp.bfloat16),
            pltpu.SMEM((masks[0].shape[0],), jnp.int32),
            pltpu.SemaphoreType.DMA,
            pltpu.SemaphoreType.DMA,
        ],
        compiler_params=ROOM,
        cost_estimate=CHEAP,
        name="lay_below",
    )(lists, counts, *masks, *panels, right, known)


def last_kernel(left_ref, right_ref, known_ref, out_ref):
    new = jnp.dot(left_ref[...], right_ref[...], preferred_element_type=jnp.float32)
    out_ref[...] = (known_ref[...] + new).astype(out_ref.dtype)


def last_product(left, right, known):
    return pl.pallas_call(
        last_kernel,
        out_shape=jax.ShapeDtypeStruct(known.shape, jnp.bfloat16),
        in_specs=[VMEM] * 3,
        out_specs=VMEM,
        compiler_params=ROOM,
        cost_estimate=CHEAP,
        name="last_product",
    )(left, right, known)


def on_device(n_row, n_col, left_blocks, left_mask, right_blocks, pair_lists, pair_counts):
    panel = left_blocks.shape[0]
    last = n_col - 1
    half = 2 * CAPM

    def shift(rows, cols, chosen):
        return [
            (r * n_col + c, (r + rows) % n_row * n_col + (c + cols) % n_col)
            for r in range(n_row)
            for c in range(n_col)
            if chosen(c)
        ]

    packed, sent_right = stage(left_mask, left_blocks, right_blocks)
    two_below = by_pairs(packed, shift(0, 2, lambda c: True))
    right_before = by_pairs(sent_right, shift(1, 0, lambda c: True))
    one_above = by_pairs(packed, shift(0, -1, lambda c: c > 0))
    one_below = by_pairs(packed, shift(0, 1, lambda c: c % RING < RING - 1))
    passed = jnp.where(lax.axis_index("pcol") == 0, packed, two_below)
    handed = by_pairs(
        passed,
        shift(0, -1, lambda c: c % RING == 1) + shift(0, -1, lambda c: c == 0),
    )

    column = lax.axis_index("pcol")
    run = jnp.int32(0)
    for q in range(mask_ref.shape[0]):
        rank_ref[q] = run
        run = run + (mask_ref[q] != 0).astype(jnp.int32)
    held = [(panel_ref, where(column)) for panel_ref, where in sources]
    total = jnp.int32(0)
    for p in range(lists_ref.shape[3]):
        block = lists_ref[0, u, 0, p]
        slot = lists_ref[0, u, 1, p]
        o = lists_ref[0, u, 2, p]
        live = jnp.logical_and(p < counts_ref[0, u], mask_ref[block] != 0)
        row = pl.multiple_of(jnp.minimum(rank_ref[block], CAP_L - 1) * BS, BS)
        down = pl.multiple_of(o * BS, BS)
        along = pl.multiple_of((at * CAPM + slot) * BS, BS)
        target = into_ref.at[pl.ds(down, BS), pl.ds(along, BS)]
        for panel_ref, here in held:
            taken = jnp.logical_and(live, here)

            @pl.when(taken)
            def _(panel_ref=panel_ref, row=row, target=target):
                pltpu.make_async_copy(panel_ref.at[pl.ds(row, BS)], target, sem).start()

            total = total + taken.astype(jnp.int32)
    return total


def drain(total, panel_ref, into_ref, sem):
    @pl.loop(0, total)
    def _(_):
        one = panel_ref.at[pl.ds(0, BS)]
        pltpu.make_async_copy(one, into_ref.at[pl.ds(0, BS), pl.ds(0, BS)], sem).wait()


def multiply(left_ref, right_ref, total_ref):
    for m in range(right_ref.shape[0]):
        total_ref[...] += jnp.dot(
            left_ref[:, m * BS : (m + 1) * BS], right_ref[m], preferred_element_type=jnp.float32
        )


def one_kernel(
    u, here, lists_ref, counts_ref, mask_ref, panel_ref, right_ref, *refs,
):
    before_ref = refs[0] if len(refs) == 7 else None
    known_ref, left_ref, held_ref, rank_ref, sem, right_sem = refs[-6:]
    fetch_right = pltpu.make_async_copy(
        right_ref.at[pl.ds((u - 2) * CAPM, CAPM)], held_ref, right_sem
    )
    fetch_right.start()
    left_ref[...] = jnp.zeros_like(left_ref)
    source = ((panel_ref, here),)
    total = place(u, 0, lists_ref, counts_ref, mask_ref, source, left_ref, rank_ref, sem)
    drain(total, panel_ref, left_ref, sem)
    fetch_right.wait()
    known_ref[...] = jnp.zeros_like(known_ref) if before_ref is None else before_ref[...]
    multiply(left_ref, held_ref, known_ref)


def one_step(u, here, lists, counts, mask, panel, right, before, cost, name):
    more = [] if before is None else [before]
    return pl.pallas_call(
        functools.partial(one_kernel, u, here),
        out_shape=jax.ShapeDtypeStruct((BR * BS, BS), jnp.float32),
        in_specs=[SMEM] * 3 + [ANY] * 2 + [VMEM] * len(more),
        out_specs=VMEM,
        scratch_shapes=[
            pltpu.VMEM((BR * BS, CAPM * BS), jnp.bfloat16),
            pltpu.VMEM((CAPM, BS, BS), jnp.bfloat16),
            pltpu.SMEM((mask.shape[0],), jnp.int32),
            pltpu.SemaphoreType.DMA,
            pltpu.SemaphoreType.DMA,
        ],
        compiler_params=ROOM,
        cost_estimate=cost,
        name=name,
    )(lists, counts, mask, panel, right, *more)


def late_kernel(
    last, lists_ref, counts_ref, two_mask_ref, one_mask_ref, handed_mask_ref,
    two_ref, one_ref, handed_ref, right_ref, early_ref,
    laid_ref, known_ref, left_ref, held_ref, rank_ref, sem, right_sem,
):
    laid_ref[...] = jnp.zeros_like(laid_ref)
    two = ((two_ref, lambda c: c >= 0),)
    one = (
        (one_ref, lambda c: lax.rem(c, RING) != 0),
        (handed_ref, lambda c: lax.rem(c, RING) == 0),
    )
    total = place(0, 0, lists_ref, counts_ref, two_mask_ref, two, laid_ref, rank_ref, sem)
    total += place(1, 1, lists_ref, counts_ref, one_mask_ref, one, laid_ref, rank_ref, sem)
    known_ref[...] = early_ref[...]
    drain(total, two_ref, laid_ref, sem)

    @pl.when(lax.axis_index("pcol") == last)
    def _():
        fetch_right = pltpu.make_async_copy(
            right_ref.at[pl.ds(CAPM, CAPM)], held_ref, right_sem
        )
        fetch_right.start()
        left_ref[...] = jnp.zeros_like(left_ref)
        above = ((handed_ref, lambda c: c >= 0),)
        count = place(
            3, 0, lists_ref, counts_ref, handed_mask_ref, above, left_ref, rank_ref, sem
        )
        drain(count, handed_ref, left_ref, sem)
        fetch_right.wait()
        multiply(left_ref, held_ref, known_ref)


def late(last, lists, counts, masks, panels, right, known):
    return pl.pallas_call(
        functools.partial(late_kernel, last),
        out_shape=[
            jax.ShapeDtypeStruct((BR * BS, 2 * CAPM * BS), jnp.bfloat16),
            jax.ShapeDtypeStruct((BR * BS, BS), jnp.float32),
        ],
        in_specs=[SMEM] * 5 + [ANY] * 4 + [VMEM],
        out_specs=[VMEM, VMEM],
        scratch_shapes=[
            pltpu.VMEM((BR * BS, CAPM * BS), jnp.bfloat16),
            pltpu.VMEM((CAPM, BS, BS), jnp.bfloat16),
            pltpu.SMEM((masks[0].shape[0],), jnp.int32),
            pltpu.SemaphoreType.DMA,
            pltpu.SemaphoreType.DMA,
        ],
        compiler_params=ROOM,
        cost_estimate=CHEAP,
        name="lay_below",
    )(lists, counts, *masks, *panels, right, known)


def last_kernel(left_ref, right_ref, known_ref, out_ref):
    new = jnp.dot(left_ref[...], right_ref[...], preferred_element_type=jnp.float32)
    out_ref[...] = (known_ref[...] + new).astype(out_ref.dtype)


def last_product(left, right, known):
    return pl.pallas_call(
        last_kernel,
        out_shape=jax.ShapeDtypeStruct(known.shape, jnp.bfloat16),
        in_specs=[VMEM] * 3,
        out_specs=VMEM,
        compiler_params=ROOM,
        cost_estimate=CHEAP,
        name="last_product",
    )(left, right, known)


def on_device(n_row, n_col, left_blocks, left_mask, right_blocks, pair_lists, pair_counts):
    panel = left_blocks.shape[0]
    last = n_col - 1
    half = 2 * CAPM

    def shift(rows, cols, chosen):
        return [
            (r * n_col + c, (r + rows) % n_row * n_col + (c + cols) % n_col)
            for r in range(n_row)
            for c in range(n_col)
            if chosen(c)
        ]

    packed, sent_right = stage(left_mask, left_blocks, right_blocks)
    two_below = by_pairs(packed, shift(0, 2, lambda c: True))
    one_above = by_pairs(packed, shift(0, -1, lambda c: c > 0))
    one_below = by_pairs(packed, shift(0, 1, lambda c: c % RING < RING - 1))
    right_before = by_pairs(sent_right, shift(1, 0, lambda c: True))
    handed = by_pairs(
        two_below,
        shift(0, -1, lambda c: c % RING == 1) + shift(0, -3, lambda c: c == 2),
    )

    column = lax.axis_index("pcol")
    mask_handed = mask_of(handed, panel)
    known = one_step(
        2, lambda c: c >= 0, pair_lists, pair_counts, left_mask, packed, right_blocks, None,
        DEAR, "own_step",
    )
    known = one_step(
        3, lambda c: c < last, pair_lists, pair_counts, mask_of(one_above, panel), one_above,
        right_blocks, known, CHEAP, "step_above",
    )
    mask_one = jnp.where(column % RING == 0, mask_handed, mask_of(one_below, panel))
    laid, known = late(
        last, pair_lists, pair_counts, [mask_of(two_below, panel), mask_one, mask_handed],
        [two_below, one_below, handed], right_blocks, known,
    )
    return last_product(laid, right_before.reshape(half * BS, BS), known)


def solution(mesh):
    in_specs = (
        P(("prow", "pcol"), None, None),
        P(("prow", "pcol")),
        P(("prow", "pcol"), None, None),
        P(("prow", "pcol"), None, None, None),
        P(("prow", "pcol"), None),
    )
    return jax.shard_map(
        functools.partial(on_device, mesh.shape["prow"], mesh.shape["pcol"]),
        mesh=mesh,
        in_specs=in_specs,
        out_specs=P("prow", "pcol"),
        check_vma=False,
    )
```

```python
import functools

import jax
import jax.numpy as jnp
from jax import lax
from jax.experimental import pallas as pl
from jax.experimental.pallas import tpu as pltpu
from jax.sharding import PartitionSpec as P

BR = 2
BS = 128
SUBS = 4
CAP_L = 19
CAPM = 6
META = 16
RING = 4
ROWS = CAP_L * BS + META
CHEAP = pl.CostEstimate(flops=0, bytes_accessed=1024, transcendentals=0)
DEAR = pl.CostEstimate(flops=1 << 35, bytes_accessed=1 << 20, transcendentals=0)
ROOM = pltpu.CompilerParams(vmem_limit_bytes=16 << 20)
SMEM = pl.BlockSpec(memory_space=pltpu.SMEM)
VMEM = pl.BlockSpec(memory_space=pltpu.VMEM)
ANY = pl.BlockSpec(memory_space=pl.ANY)


def by_pairs(array, pairs):
    return lax.ppermute(array, ("prow", "pcol"), pairs)


def stage_kernel(mask_ref, left_ref, right_ref, packed_ref, part_ref, sem, part_sem):
    panel = left_ref.shape[0]
    half = part_ref.shape[0]
    part = pltpu.make_async_copy(right_ref.at[pl.ds(half, half)], part_ref, part_sem)
    part.start()
    slot = jnp.int32(0)
    for q in range(panel):
        taken = jnp.logical_and(mask_ref[q] != 0, slot < CAP_L)

        @pl.when(taken)
        def _(q=q, slot=slot):
            row = pl.multiple_of(slot * BS, BS)
            pltpu.make_async_copy(left_ref.at[q], packed_ref.at[pl.ds(row, BS)], sem).start()

        slot = slot + taken.astype(jnp.int32)

    @pl.loop(slot, CAP_L)
    def _(spare):
        row = pl.multiple_of(spare * BS, BS)
        pltpu.make_async_copy(left_ref.at[0], packed_ref.at[pl.ds(row, BS)], sem).start()

    lane = lax.broadcasted_iota(jnp.int32, (META, BS), 1)
    mask = jnp.zeros((META, BS), jnp.float32)
    for q in range(panel):
        mask = jnp.where(lane == q, (mask_ref[q] != 0).astype(jnp.float32), mask)
    packed_ref[pl.ds(CAP_L * BS, META), :] = mask.astype(packed_ref.dtype)
    blocks = packed_ref.at[pl.ds(0, CAP_L * BS)]
    pltpu.make_async_copy(blocks, blocks, sem).wait()
    part.wait()


def stage(left_mask, left_blocks, right_blocks):
    return pl.pallas_call(
        stage_kernel,
        out_shape=[
            jax.ShapeDtypeStruct((CAP_L * BS + META, BS), jnp.bfloat16),
            jax.ShapeDtypeStruct((2 * CAPM, BS, BS), jnp.bfloat16),
        ],
        in_specs=[SMEM, ANY, ANY],
        out_specs=[VMEM, VMEM],
        scratch_shapes=[pltpu.SemaphoreType.DMA, pltpu.SemaphoreType.DMA],
        compiler_params=pltpu.CompilerParams(vmem_limit_bytes=62 << 20),
        cost_estimate=CHEAP,
        name="pack_and_cut",
    )(left_mask, left_blocks, right_blocks)


def mask_of(packed, panel):
    return packed[CAP_L * BS, :panel].astype(jnp.int32)


def place(u, at, lists_ref, counts_ref, mask_ref, sources, into_ref, rank_ref, sem):
    column = lax.axis_index("pcol")
    run = jnp.int32(0)
    for q in range(mask_ref.shape[0]):
        rank_ref[q] = run
        run = run + (mask_ref[q] != 0).astype(jnp.int32)
    held = [(panel_ref, where(column), base(column)) for panel_ref, where, base in sources]
    total = jnp.int32(0)
    for p in range(lists_ref.shape[3]):
        block = lists_ref[0, u, 0, p]
        slot = lists_ref[0, u, 1, p]
        o = lists_ref[0, u, 2, p]
        live = jnp.logical_and(p < counts_ref[0, u], mask_ref[block] != 0)
        row = jnp.minimum(rank_ref[block], CAP_L - 1) * BS
        down = pl.multiple_of(o * BS, BS)
        along = pl.multiple_of((at * CAPM + slot) * BS, BS)
        target = into_ref.at[pl.ds(down, BS), pl.ds(along, BS)]
        for panel_ref, here, base in held:
            taken = jnp.logical_and(live, here)
            first = pl.multiple_of(row + base * ROWS, META)

            @pl.when(taken)
            def _(panel_ref=panel_ref, first=first, target=target):
                pltpu.make_async_copy(panel_ref.at[pl.ds(first, BS)], target, sem).start()

            total = total + taken.astype(jnp.int32)
    return total


def drain(total, panel_ref, into_ref, sem):
    @pl.loop(0, total)
    def _(_):
        one = panel_ref.at[pl.ds(0, BS)]
        pltpu.make_async_copy(one, into_ref.at[pl.ds(0, BS), pl.ds(0, BS)], sem).wait()


def multiply(left_ref, right_ref, total_ref):
    for m in range(right_ref.shape[0]):
        total_ref[...] += jnp.dot(
            left_ref[:, m * BS : (m + 1) * BS], right_ref[m], preferred_element_type=jnp.float32
        )


def zero(c):
    return 0


def own_kernel(
    lists_ref, counts_ref, mask_ref, panel_ref, right_ref,
    known_ref, left_ref, held_ref, rank_ref, sem, right_sem,
):
    fetch_right = pltpu.make_async_copy(right_ref.at[pl.ds(0, CAPM)], held_ref, right_sem)
    fetch_right.start()
    left_ref[...] = jnp.zeros_like(left_ref)
    own = ((panel_ref, lambda c: c >= 0, zero),)
    total = place(2, 0, lists_ref, counts_ref, mask_ref, own, left_ref, rank_ref, sem)
    drain(total, panel_ref, left_ref, sem)
    fetch_right.wait()
    known_ref[...] = jnp.zeros_like(known_ref)
    multiply(left_ref, held_ref, known_ref)


def scratch(panel):
    return [
        pltpu.VMEM((BR * BS, CAPM * BS), jnp.bfloat16),
        pltpu.VMEM((CAPM, BS, BS), jnp.bfloat16),
        pltpu.SMEM((panel,), jnp.int32),
        pltpu.SemaphoreType.DMA,
        pltpu.SemaphoreType.DMA,
    ]


def own_step(lists, counts, mask, packed, right):
    return pl.pallas_call(
        own_kernel,
        out_shape=jax.ShapeDtypeStruct((BR * BS, BS), jnp.float32),
        in_specs=[SMEM] * 3 + [ANY] * 2,
        out_specs=VMEM,
        scratch_shapes=scratch(mask.shape[0]),
        compiler_params=ROOM,
        cost_estimate=DEAR,
        name="own_step",
    )(lists, counts, mask, packed, right)


def late_kernel(
    last, lists_ref, counts_ref, two_mask_ref, one_mask_ref, above_mask_ref,
    row_ref, crossed_ref, handed_ref, around_ref, right_ref, own_ref,
    laid_ref, known_ref, left_ref, held_ref, rank_ref, sem, right_sem,
):
    fetch_right = pltpu.make_async_copy(right_ref.at[pl.ds(CAPM, CAPM)], held_ref, right_sem)
    fetch_right.start()
    laid_ref[...] = jnp.zeros_like(laid_ref)
    left_ref[...] = jnp.zeros_like(left_ref)

    def at(c):
        return lax.rem(c, RING)

    two = (
        (row_ref, lambda c: at(c) >= 2, lambda c: jnp.maximum(at(c) - 2, 0)),
        (crossed_ref, lambda c: at(c) < 2, zero),
    )
    one = (
        (row_ref, lambda c: at(c) >= 1, lambda c: jnp.maximum(at(c) - 1, 0)),
        (handed_ref, lambda c: at(c) == 0, zero),
    )
    above = (
        (row_ref, lambda c: at(c) < RING - 1, lambda c: jnp.minimum(at(c) + 1, RING - 1)),
        (crossed_ref, lambda c: jnp.logical_and(at(c) == RING - 1, c != last), zero),
        (around_ref, lambda c: c == last, zero),
    )
    total = place(0, 0, lists_ref, counts_ref, two_mask_ref, two, laid_ref, rank_ref, sem)
    total += place(1, 1, lists_ref, counts_ref, one_mask_ref, one, laid_ref, rank_ref, sem)
    total += place(3, 0, lists_ref, counts_ref, above_mask_ref, above, left_ref, rank_ref, sem)
    known_ref[...] = own_ref[...]
    drain(total, crossed_ref, laid_ref, sem)
    fetch_right.wait()
    multiply(left_ref, held_ref, known_ref)


def late(last, lists, counts, masks, panels, right, known):
    return pl.pallas_call(
        functools.partial(late_kernel, last),
        out_shape=[
            jax.ShapeDtypeStruct((BR * BS, 2 * CAPM * BS), jnp.bfloat16),
            jax.ShapeDtypeStruct((BR * BS, BS), jnp.float32),
        ],
        in_specs=[SMEM] * 5 + [ANY] * 5 + [VMEM],
        out_specs=[VMEM, VMEM],
        scratch_shapes=scratch(masks[0].shape[0]),
        compiler_params=ROOM,
        cost_estimate=CHEAP,
        name="other_steps",
    )(lists, counts, *masks, *panels, right, known)


def last_kernel(left_ref, right_ref, known_ref, out_ref):
    new = jnp.dot(left_ref[...], right_ref[...], preferred_element_type=jnp.float32)
    out_ref[...] = (known_ref[...] + new).astype(out_ref.dtype)


def last_product(left, right, known):
    return pl.pallas_call(
        last_kernel,
        out_shape=jax.ShapeDtypeStruct(known.shape, jnp.bfloat16),
        in_specs=[VMEM] * 3,
        out_specs=VMEM,
        compiler_params=ROOM,
        cost_estimate=CHEAP,
        name="last_product",
    )(left, right, known)


def on_device(n_row, n_col, left_blocks, left_mask, right_blocks, pair_lists, pair_counts):
    panel = left_blocks.shape[0]
    last = n_col - 1
    half = 2 * CAPM

    def shift(rows, cols, chosen):
        return [
            (r * n_col + c, (r + rows) % n_row * n_col + (c + cols) % n_col)
            for r in range(n_row)
            for c in range(n_col)
            if chosen(c)
        ]

    packed, sent_right = stage(left_mask, left_blocks, right_blocks)
    crossed = by_pairs(
        packed,
        shift(0, 2, lambda c: c % RING >= 2)
        + shift(0, -1, lambda c: c % RING == 0 and c != 0),
    )
    rings = [[first + at for at in range(RING)] for first in range(0, n_col, RING)]
    row = lax.all_gather(packed, "pcol", axis_index_groups=rings)
    right_before = by_pairs(sent_right, shift(1, 0, lambda c: True))
    handed = by_pairs(crossed, shift(0, -1, lambda c: c % RING == 1))
    around = by_pairs(row[0], shift(0, -2, lambda c: c == 1))

    column = lax.axis_index("pcol")
    place_in_row = column % RING
    row_masks = row[:, CAP_L * BS, :panel].astype(jnp.int32)

    def row_mask(step):
        return row_masks[(place_in_row + step) % RING]

    crossed_mask = mask_of(crossed, panel)
    masks = [
        jnp.where(place_in_row >= 2, row_mask(-2), crossed_mask),
        jnp.where(place_in_row >= 1, row_mask(-1), mask_of(handed, panel)),
        jnp.where(
            column == last,
            mask_of(around, panel),
            jnp.where(place_in_row < RING - 1, row_mask(1), crossed_mask),
        ),
    ]
    known = own_step(pair_lists, pair_counts, left_mask, packed, right_blocks)
    laid, known = late(
        last, pair_lists, pair_counts, masks,
        [row.reshape(RING * ROWS, BS), crossed, handed, around], right_blocks, known,
    )
    return last_product(laid, right_before.reshape(half * BS, BS), known)


def solution(mesh):
    in_specs = (
        P(("prow", "pcol"), None, None),
        P(("prow", "pcol")),
        P(("prow", "pcol"), None, None),
        P(("prow", "pcol"), None, None, None),
        P(("prow", "pcol"), None),
    )
    return jax.shard_map(
        functools.partial(on_device, mesh.shape["prow"], mesh.shape["pcol"]),
        mesh=mesh,
        in_specs=in_specs,
        out_specs=P("prow", "pcol"),
        check_vma=False,
    )
```

```python
import functools

import jax
import jax.numpy as jnp
from jax import lax
from jax.experimental import pallas as pl
from jax.experimental.pallas import tpu as pltpu
from jax.sharding import PartitionSpec as P

BR = 2
BS = 128
CAP_L = 19
CAPM = 6
PCAP = 12
META = 16
RING = 4
CHEAP = pl.CostEstimate(flops=0, bytes_accessed=1024, transcendentals=0)
DEAR = pl.CostEstimate(flops=1 << 35, bytes_accessed=1 << 20, transcendentals=0)
ROOM = pltpu.CompilerParams(vmem_limit_bytes=16 << 20)
WIDE = pltpu.CompilerParams(vmem_limit_bytes=62 << 20)
SMEM = pl.BlockSpec(memory_space=pltpu.SMEM)
VMEM = pl.BlockSpec(memory_space=pltpu.VMEM)
ANY = pl.BlockSpec(memory_space=pl.ANY)


def by_pairs(array, pairs):
    return lax.ppermute(array, ("prow", "pcol"), pairs)


def pack_into(mask_ref, left_ref, packed_ref, sem):
    panel = left_ref.shape[0]
    slot = jnp.int32(0)
    for q in range(panel):
        taken = jnp.logical_and(mask_ref[q] != 0, slot < CAP_L)

        @pl.when(taken)
        def _(q=q, slot=slot):
            row = pl.multiple_of(slot * BS, BS)
            pltpu.make_async_copy(left_ref.at[q], packed_ref.at[pl.ds(row, BS)], sem).start()

        slot = slot + taken.astype(jnp.int32)

    @pl.loop(slot, CAP_L)
    def _(spare):
        row = pl.multiple_of(spare * BS, BS)
        pltpu.make_async_copy(left_ref.at[0], packed_ref.at[pl.ds(row, BS)], sem).start()

    lane = lax.broadcasted_iota(jnp.int32, (META, BS), 1)
    mask = jnp.zeros((META, BS), jnp.float32)
    for q in range(panel):
        mask = jnp.where(lane == q, (mask_ref[q] != 0).astype(jnp.float32), mask)
    packed_ref[pl.ds(CAP_L * BS, META), :] = mask.astype(packed_ref.dtype)


def wait_packed(packed_ref, sem):
    blocks = packed_ref.at[pl.ds(0, CAP_L * BS)]
    pltpu.make_async_copy(blocks, blocks, sem).wait()


def first_kernel(
    mask_ref, lists_ref, counts_ref, left_ref, right_ref,
    packed_ref, part_ref, ask_ref, sem, part_sem, ask_sem,
):
    half = part_ref.shape[0]
    part = pltpu.make_async_copy(right_ref.at[pl.ds(half, half)], part_ref, part_sem)
    part.start()
    pack_into(mask_ref, left_ref, packed_ref, sem)
    copies = []
    for m in range(CAPM):
        target = ask_ref.at[pl.ds(m * BS, BS)]
        copies.append(pltpu.make_async_copy(right_ref.at[CAPM + m], target, ask_sem.at[m]))
        copies[-1].start()
    lane = lax.broadcasted_iota(jnp.int32, (META, BS), 1)
    pairs = lists_ref.shape[3]
    row = jnp.where(lane == 3 * pairs, counts_ref[0, 3].astype(jnp.float32), 0.0)
    for q in range(3 * pairs):
        row = jnp.where(lane == q, lists_ref[0, 3, q // pairs, q % pairs].astype(jnp.float32), row)
    ask_ref[pl.ds(CAPM * BS, META), :] = row.astype(ask_ref.dtype)
    wait_packed(packed_ref, sem)
    part.wait()
    for copy in copies:
        copy.wait()


def second_kernel(mask_ref, left_ref, after_ref, packed_ref, sem):
    del after_ref
    pack_into(mask_ref, left_ref, packed_ref, sem)
    wait_packed(packed_ref, sem)


def first_stage(left_mask, lists, counts, left_blocks, right_blocks):
    return pl.pallas_call(
        first_kernel,
        out_shape=[
            jax.ShapeDtypeStruct((CAP_L * BS + META, BS), jnp.bfloat16),
            jax.ShapeDtypeStruct((2 * CAPM, BS, BS), jnp.bfloat16),
            jax.ShapeDtypeStruct((CAPM * BS + META, BS), jnp.bfloat16),
        ],
        in_specs=[SMEM] * 3 + [ANY] * 2,
        out_specs=[VMEM] * 3,
        scratch_shapes=[
            pltpu.SemaphoreType.DMA, pltpu.SemaphoreType.DMA, pltpu.SemaphoreType.DMA((CAPM,))
        ],
        compiler_params=WIDE,
        cost_estimate=CHEAP,
        name="pack_and_cut",
    )(left_mask, lists, counts, left_blocks, right_blocks)


def second_stage(left_mask, left_blocks, after):
    return pl.pallas_call(
        second_kernel,
        out_shape=jax.ShapeDtypeStruct((CAP_L * BS + META, BS), jnp.bfloat16),
        in_specs=[SMEM, ANY, ANY],
        out_specs=VMEM,
        scratch_shapes=[pltpu.SemaphoreType.DMA],
        compiler_params=WIDE,
        cost_estimate=CHEAP,
        name="pack_again",
    )(left_mask, left_blocks, after)


def mask_of(packed, panel):
    return packed[CAP_L * BS, :panel].astype(jnp.int32)


def place(u, at, lists_ref, counts_ref, mask_ref, sources, into_ref, rank_ref, sem):
    column = lax.axis_index("pcol")
    run = jnp.int32(0)
    for q in range(mask_ref.shape[0]):
        rank_ref[q] = run
        run = run + (mask_ref[q] != 0).astype(jnp.int32)
    held = [(panel_ref, where(column)) for panel_ref, where in sources]
    total = jnp.int32(0)
    for p in range(lists_ref.shape[3]):
        block = lists_ref[0, u, 0, p]
        slot = lists_ref[0, u, 1, p]
        o = lists_ref[0, u, 2, p]
        live = jnp.logical_and(p < counts_ref[0, u], mask_ref[block] != 0)
        row = pl.multiple_of(jnp.minimum(rank_ref[block], CAP_L - 1) * BS, BS)
        down = pl.multiple_of(o * BS, BS)
        along = pl.multiple_of((at * CAPM + slot) * BS, BS)
        target = into_ref.at[pl.ds(down, BS), pl.ds(along, BS)]
        for panel_ref, here in held:
            taken = jnp.logical_and(live, here)

            @pl.when(taken)
            def _(panel_ref=panel_ref, row=row, target=target):
                pltpu.make_async_copy(panel_ref.at[pl.ds(row, BS)], target, sem).start()

            total = total + taken.astype(jnp.int32)
    return total


def drain(total, panel_ref, into_ref, sem):
    @pl.loop(0, total)
    def _(_):
        one = panel_ref.at[pl.ds(0, BS)]
        pltpu.make_async_copy(one, into_ref.at[pl.ds(0, BS), pl.ds(0, BS)], sem).wait()


def multiply(left_ref, right_ref, total_ref):
    for m in range(right_ref.shape[0]):
        total_ref[...] += jnp.dot(
            left_ref[:, m * BS : (m + 1) * BS], right_ref[m], preferred_element_type=jnp.float32
        )


def one_kernel(
    u, first, here, lists_ref, counts_ref, mask_ref, panel_ref, right_ref, *refs,
):
    before_ref = refs[0] if len(refs) == 7 else None
    known_ref, left_ref, held_ref, rank_ref, sem, right_sem = refs[-6:]
    fetch_right = pltpu.make_async_copy(
        right_ref.at[pl.ds(first, CAPM)], held_ref, right_sem
    )
    fetch_right.start()
    left_ref[...] = jnp.zeros_like(left_ref)
    source = ((panel_ref, here),)
    total = place(u, 0, lists_ref, counts_ref, mask_ref, source, left_ref, rank_ref, sem)
    drain(total, panel_ref, left_ref, sem)
    fetch_right.wait()
    known_ref[...] = jnp.zeros_like(known_ref) if before_ref is None else before_ref[...]
    multiply(left_ref, held_ref, known_ref)


def one_step(u, first, here, lists, counts, mask, panel, right, before, cost, name):
    more = [] if before is None else [before]
    return pl.pallas_call(
        functools.partial(one_kernel, u, first, here),
        out_shape=jax.ShapeDtypeStruct((BR * BS, BS), jnp.float32),
        in_specs=[SMEM] * 3 + [ANY] * 2 + [VMEM] * len(more),
        out_specs=VMEM,
        scratch_shapes=[
            pltpu.VMEM((BR * BS, CAPM * BS), jnp.bfloat16),
            pltpu.VMEM((CAPM, BS, BS), jnp.bfloat16),
            pltpu.SMEM((mask.shape[0],), jnp.int32),
            pltpu.SemaphoreType.DMA,
            pltpu.SemaphoreType.DMA,
        ],
        compiler_params=ROOM,
        cost_estimate=cost,
        name=name,
    )(lists, counts, mask, panel, right, *more)


def late_kernel(
    lists_ref, counts_ref, two_mask_ref, one_mask_ref, two_ref, one_ref, handed_ref,
    early_ref, answer_ref, laid_ref, known_ref, rank_ref, sem,
):
    laid_ref[...] = jnp.zeros_like(laid_ref)
    two = ((two_ref, lambda c: c >= 0),)
    one = (
        (one_ref, lambda c: lax.rem(c, RING) != 0),
        (handed_ref, lambda c: lax.rem(c, RING) == 0),
    )
    total = place(0, 0, lists_ref, counts_ref, two_mask_ref, two, laid_ref, rank_ref, sem)
    total += place(1, 1, lists_ref, counts_ref, one_mask_ref, one, laid_ref, rank_ref, sem)
    known_ref[...] = early_ref[...] + answer_ref[...]
    drain(total, two_ref, laid_ref, sem)


def late(lists, counts, masks, panels, known, answer):
    return pl.pallas_call(
        late_kernel,
        out_shape=[
            jax.ShapeDtypeStruct((BR * BS, 2 * CAPM * BS), jnp.bfloat16),
            jax.ShapeDtypeStruct((BR * BS, BS), jnp.float32),
        ],
        in_specs=[SMEM] * 4 + [ANY] * 3 + [VMEM] * 2,
        out_specs=[VMEM, VMEM],
        scratch_shapes=[pltpu.SMEM((masks[0].shape[0],), jnp.int32), pltpu.SemaphoreType.DMA],
        compiler_params=ROOM,
        cost_estimate=CHEAP,
        name="lay_below",
    )(lists, counts, *masks, *panels, known, answer)


def last_kernel(left_ref, right_ref, known_ref, out_ref):
    new = jnp.dot(left_ref[...], right_ref[...], preferred_element_type=jnp.float32)
    out_ref[...] = (known_ref[...] + new).astype(out_ref.dtype)


def last_product(left, right, known):
    return pl.pallas_call(
        last_kernel,
        out_shape=jax.ShapeDtypeStruct(known.shape, jnp.bfloat16),
        in_specs=[VMEM] * 3,
        out_specs=VMEM,
        compiler_params=ROOM,
        cost_estimate=CHEAP,
        name="last_product",
    )(left, right, known)


def on_device(n_row, n_col, left_blocks, left_mask, right_blocks, pair_lists, pair_counts):
    panel = left_blocks.shape[0]
    last = n_col - 1
    half = 2 * CAPM

    def shift(rows, cols, chosen):
        return [
            (r * n_col + c, (r + rows) % n_row * n_col + (c + cols) % n_col)
            for r in range(n_row)
            for c in range(n_col)
            if chosen(c)
        ]

    def always(c):
        return c >= 0

    packed, sent_right, ask = first_stage(
        left_mask, pair_lists, pair_counts, left_blocks, right_blocks
    )
    two_below = by_pairs(packed, shift(0, 2, always))
    right_before = by_pairs(sent_right, shift(1, 0, always))
    mark = by_pairs(packed[:META], [(0, 1)])
    again = second_stage(left_mask, left_blocks, mark)
    one_above = by_pairs(again, shift(0, -1, lambda c: c > 0))
    one_below = by_pairs(again, shift(0, 1, lambda c: c % RING < RING - 1))
    asked = by_pairs(ask, shift(0, 1, lambda c: c == last))
    handed = by_pairs(two_below, shift(0, -1, lambda c: c % RING == 1))

    listed = asked[CAPM * BS, : 3 * PCAP + 1].astype(jnp.int32)
    answer = one_step(
        0, 0, always, listed[: 3 * PCAP].reshape(1, 1, 3, PCAP), listed[3 * PCAP :].reshape(1, 1),
        left_mask, packed, asked[: CAPM * BS].reshape(CAPM, BS, BS), None, CHEAP, "answer",
    )
    answer = by_pairs(answer, shift(0, -1, lambda c: c == 0))

    known = one_step(
        2, 0, always, pair_lists, pair_counts, left_mask, packed, right_blocks, None,
        DEAR, "own_step",
    )
    known = one_step(
        3, CAPM, lambda c: c < last, pair_lists, pair_counts, mask_of(one_above, panel),
        one_above, right_blocks, known, CHEAP, "step_above",
    )
    first = lax.axis_index("pcol") % RING == 0
    mask_one = jnp.where(first, mask_of(handed, panel), mask_of(one_below, panel))
    laid, known = late(
        pair_lists, pair_counts, [mask_of(two_below, panel), mask_one],
        [two_below, one_below, handed], known, answer,
    )
    return last_product(laid, right_before.reshape(half * BS, BS), known)


def solution(mesh):
    in_specs = (
        P(("prow", "pcol"), None, None),
        P(("prow", "pcol")),
        P(("prow", "pcol"), None, None),
        P(("prow", "pcol"), None, None, None),
        P(("prow", "pcol"), None),
    )
    return jax.shard_map(
        functools.partial(on_device, mesh.shape["prow"], mesh.shape["pcol"]),
        mesh=mesh,
        in_specs=in_specs,
        out_specs=P("prow", "pcol"),
        check_vma=False,
    )
```

```python
import functools

import jax
import jax.numpy as jnp
from jax import lax
from jax.experimental import pallas as pl
from jax.experimental.pallas import tpu as pltpu
from jax.sharding import PartitionSpec as P

BR = 2
BS = 128
CAP_L = 19
CAPM = 6
META = 16
RING = 4
CHEAP = pl.CostEstimate(flops=0, bytes_accessed=1024, transcendentals=0)
DEAR = pl.CostEstimate(flops=1 << 35, bytes_accessed=1 << 20, transcendentals=0)
ROOM = pltpu.CompilerParams(vmem_limit_bytes=16 << 20)
WIDE = pltpu.CompilerParams(vmem_limit_bytes=62 << 20)
SMEM = pl.BlockSpec(memory_space=pltpu.SMEM)
VMEM = pl.BlockSpec(memory_space=pltpu.VMEM)
ANY = pl.BlockSpec(memory_space=pl.ANY)


def by_pairs(array, pairs):
    return lax.ppermute(array, ("prow", "pcol"), pairs)


def pack_into(mask_ref, left_ref, packed_ref, sem):
    panel = left_ref.shape[0]
    slot = jnp.int32(0)
    for q in range(panel):
        taken = jnp.logical_and(mask_ref[q] != 0, slot < CAP_L)

        @pl.when(taken)
        def _(q=q, slot=slot):
            row = pl.multiple_of(slot * BS, BS)
            pltpu.make_async_copy(left_ref.at[q], packed_ref.at[pl.ds(row, BS)], sem).start()

        slot = slot + taken.astype(jnp.int32)

    @pl.loop(slot, CAP_L)
    def _(spare):
        row = pl.multiple_of(spare * BS, BS)
        pltpu.make_async_copy(left_ref.at[0], packed_ref.at[pl.ds(row, BS)], sem).start()

    lane = lax.broadcasted_iota(jnp.int32, (META, BS), 1)
    mask = jnp.zeros((META, BS), jnp.float32)
    for q in range(panel):
        mask = jnp.where(lane == q, (mask_ref[q] != 0).astype(jnp.float32), mask)
    packed_ref[pl.ds(CAP_L * BS, META), :] = mask.astype(packed_ref.dtype)


def wait_packed(packed_ref, sem):
    blocks = packed_ref.at[pl.ds(0, CAP_L * BS)]
    pltpu.make_async_copy(blocks, blocks, sem).wait()


def cut_kernel(right_ref, after_ref, part_ref, sem):
    del after_ref
    half = part_ref.shape[0]
    part = pltpu.make_async_copy(right_ref.at[pl.ds(half, half)], part_ref, sem)
    part.start()
    part.wait()


def cut(right_blocks, after):
    return pl.pallas_call(
        cut_kernel,
        out_shape=jax.ShapeDtypeStruct((2 * CAPM, BS, BS), jnp.bfloat16),
        in_specs=[ANY, ANY],
        out_specs=VMEM,
        scratch_shapes=[pltpu.SemaphoreType.DMA],
        compiler_params=WIDE,
        cost_estimate=CHEAP,
        name="cut_right",
    )(right_blocks, after)


def pack_kernel(mask_ref, left_ref, after_ref, packed_ref, sem):
    del after_ref
    pack_into(mask_ref, left_ref, packed_ref, sem)
    wait_packed(packed_ref, sem)


def pack(left_mask, left_blocks, after, name):
    return pl.pallas_call(
        pack_kernel,
        out_shape=jax.ShapeDtypeStruct((CAP_L * BS + META, BS), jnp.bfloat16),
        in_specs=[SMEM, ANY, ANY],
        out_specs=VMEM,
        scratch_shapes=[pltpu.SemaphoreType.DMA],
        compiler_params=WIDE,
        cost_estimate=CHEAP,
        name=name,
    )(left_mask, left_blocks, after)


def mask_of(packed, panel):
    return packed[CAP_L * BS, :panel].astype(jnp.int32)


def place(u, at, lists_ref, counts_ref, mask_ref, sources, into_ref, rank_ref, sem):
    column = lax.axis_index("pcol")
    run = jnp.int32(0)
    for q in range(mask_ref.shape[0]):
        rank_ref[q] = run
        run = run + (mask_ref[q] != 0).astype(jnp.int32)
    held = [(panel_ref, where(column)) for panel_ref, where in sources]
    total = jnp.int32(0)
    for p in range(lists_ref.shape[3]):
        block = lists_ref[0, u, 0, p]
        slot = lists_ref[0, u, 1, p]
        o = lists_ref[0, u, 2, p]
        live = jnp.logical_and(p < counts_ref[0, u], mask_ref[block] != 0)
        row = pl.multiple_of(jnp.minimum(rank_ref[block], CAP_L - 1) * BS, BS)
        down = pl.multiple_of(o * BS, BS)
        along = pl.multiple_of((at * CAPM + slot) * BS, BS)
        target = into_ref.at[pl.ds(down, BS), pl.ds(along, BS)]
        for panel_ref, here in held:
            taken = jnp.logical_and(live, here)

            @pl.when(taken)
            def _(panel_ref=panel_ref, row=row, target=target):
                pltpu.make_async_copy(panel_ref.at[pl.ds(row, BS)], target, sem).start()

            total = total + taken.astype(jnp.int32)
    return total


def drain(total, panel_ref, into_ref, sem):
    @pl.loop(0, total)
    def _(_):
        one = panel_ref.at[pl.ds(0, BS)]
        pltpu.make_async_copy(one, into_ref.at[pl.ds(0, BS), pl.ds(0, BS)], sem).wait()


def multiply(left_ref, right_ref, total_ref):
    for m in range(right_ref.shape[0]):
        total_ref[...] += jnp.dot(
            left_ref[:, m * BS : (m + 1) * BS], right_ref[m], preferred_element_type=jnp.float32
        )


def one_kernel(
    u, first, here, lists_ref, counts_ref, mask_ref, panel_ref, right_ref, *refs,
):
    before_ref = refs[0] if len(refs) == 7 else None
    known_ref, left_ref, held_ref, rank_ref, sem, right_sem = refs[-6:]
    fetch_right = pltpu.make_async_copy(
        right_ref.at[pl.ds(first, CAPM)], held_ref, right_sem
    )
    fetch_right.start()
    left_ref[...] = jnp.zeros_like(left_ref)
    source = ((panel_ref, here),)
    total = place(u, 0, lists_ref, counts_ref, mask_ref, source, left_ref, rank_ref, sem)
    drain(total, panel_ref, left_ref, sem)
    fetch_right.wait()
    known_ref[...] = jnp.zeros_like(known_ref) if before_ref is None else before_ref[...]
    multiply(left_ref, held_ref, known_ref)


def one_step(u, first, here, lists, counts, mask, panel, right, before, cost, name):
    more = [] if before is None else [before]
    return pl.pallas_call(
        functools.partial(one_kernel, u, first, here),
        out_shape=jax.ShapeDtypeStruct((BR * BS, BS), jnp.float32),
        in_specs=[SMEM] * 3 + [ANY] * 2 + [VMEM] * len(more),
        out_specs=VMEM,
        scratch_shapes=[
            pltpu.VMEM((BR * BS, CAPM * BS), jnp.bfloat16),
            pltpu.VMEM((CAPM, BS, BS), jnp.bfloat16),
            pltpu.SMEM((mask.shape[0],), jnp.int32),
            pltpu.SemaphoreType.DMA,
            pltpu.SemaphoreType.DMA,
        ],
        compiler_params=ROOM,
        cost_estimate=cost,
        name=name,
    )(lists, counts, mask, panel, right, *more)


def late_kernel(
    lists_ref, counts_ref, one_mask_ref, two_mask_ref,
    two_ref, wrapped_ref, one_ref, handed_ref, laid_ref, rank_ref, sem,
):
    laid_ref[...] = jnp.zeros_like(laid_ref)
    two = ((two_ref, lambda c: c >= 2), (wrapped_ref, lambda c: c < 2))
    one = (
        (one_ref, lambda c: lax.rem(c, RING) != 0),
        (handed_ref, lambda c: lax.rem(c, RING) == 0),
    )
    total = place(0, 0, lists_ref, counts_ref, two_mask_ref, two, laid_ref, rank_ref, sem)
    total += place(1, 1, lists_ref, counts_ref, one_mask_ref, one, laid_ref, rank_ref, sem)
    drain(total, two_ref, laid_ref, sem)


def late(lists, counts, masks, panels):
    return pl.pallas_call(
        late_kernel,
        out_shape=jax.ShapeDtypeStruct((BR * BS, 2 * CAPM * BS), jnp.bfloat16),
        in_specs=[SMEM] * 4 + [ANY] * 4,
        out_specs=VMEM,
        scratch_shapes=[pltpu.SMEM((masks[0].shape[0],), jnp.int32), pltpu.SemaphoreType.DMA],
        compiler_params=ROOM,
        cost_estimate=CHEAP,
        name="lay_below",
    )(lists, counts, *masks, *panels)


def pass_kernel(two_ref, wrapped_ref, after_ref, passed_ref, sem):
    del after_ref
    column = lax.axis_index("pcol")

    @pl.when(column == 1)
    def _():
        copy = pltpu.make_async_copy(wrapped_ref, passed_ref, sem)
        copy.start()
        copy.wait()

    @pl.when(jnp.logical_and(column != 1, lax.rem(column, RING) == 1))
    def _():
        copy = pltpu.make_async_copy(two_ref, passed_ref, sem)
        copy.start()
        copy.wait()


def pass_on(two_below, wrapped, after):
    return pl.pallas_call(
        pass_kernel,
        out_shape=jax.ShapeDtypeStruct(two_below.shape, two_below.dtype),
        in_specs=[ANY] * 3,
        out_specs=VMEM,
        scratch_shapes=[pltpu.SemaphoreType.DMA],
        compiler_params=ROOM,
        cost_estimate=CHEAP,
        name="pass_on",
    )(two_below, wrapped, after)


def last_kernel(known_ref, left_ref, right_ref, out_ref):
    new = jnp.dot(left_ref[...], right_ref[...], preferred_element_type=jnp.float32)
    out_ref[...] = (known_ref[...] + new).astype(out_ref.dtype)


def last_product(known, left, right):
    return pl.pallas_call(
        last_kernel,
        out_shape=jax.ShapeDtypeStruct(known.shape, jnp.bfloat16),
        in_specs=[VMEM] * 3,
        out_specs=VMEM,
        compiler_params=ROOM,
        cost_estimate=CHEAP,
        name="last_product",
    )(known, left, right)


def on_device(n_row, n_col, left_blocks, left_mask, right_blocks, pair_lists, pair_counts):
    panel = left_blocks.shape[0]
    last = n_col - 1
    half = 2 * CAPM

    def shift(rows, cols, chosen):
        return [
            (r * n_col + c, (r + rows) % n_row * n_col + (c + cols) % n_col)
            for r in range(n_row)
            for c in range(n_col)
            if chosen(c)
        ]

    def always(c):
        return c >= 0

    column = lax.axis_index("pcol")
    mark = by_pairs(left_mask, [(0, 1)])
    mark_again = by_pairs(mark, [(1, 0)])
    packed = pack(left_mask, left_blocks, left_mask, "pack_panel")
    wrapped = by_pairs(packed, shift(0, 2, lambda c: c >= last - 1))
    right_before = by_pairs(cut(right_blocks, mark), shift(1, 0, always))
    again = pack(left_mask, left_blocks, mark_again, "pack_again")
    two_below = by_pairs(again, shift(0, 2, lambda c: c < last - 1))
    one_above = by_pairs(again, shift(0, -1, always))
    one_below = by_pairs(again, shift(0, 1, lambda c: c % RING < RING - 1))
    known = one_step(
        2, 0, always, pair_lists, pair_counts, left_mask, again, right_blocks, None,
        DEAR, "own_step",
    )
    passed = pass_on(two_below, wrapped, known)
    handed = by_pairs(passed, shift(0, -1, lambda c: c % RING == 1))
    known = one_step(
        3, CAPM, always, pair_lists, pair_counts, mask_of(one_above, panel),
        one_above, right_blocks, known, DEAR, "step_above",
    )
    mask_two = jnp.where(column < 2, mask_of(wrapped, panel), mask_of(two_below, panel))
    mask_one = jnp.where(
        column % RING != 0, mask_of(one_below, panel), mask_of(handed, panel)
    )
    laid = late(
        pair_lists, pair_counts, [mask_one, mask_two],
        [two_below, wrapped, one_below, handed],
    )
    return last_product(known, laid, right_before.reshape(half * BS, BS))


def solution(mesh):
    in_specs = (
        P(("prow", "pcol"), None, None),
        P(("prow", "pcol")),
        P(("prow", "pcol"), None, None),
        P(("prow", "pcol"), None, None, None),
        P(("prow", "pcol"), None),
    )
    return jax.shard_map(
        functools.partial(on_device, mesh.shape["prow"], mesh.shape["pcol"]),
        mesh=mesh,
        in_specs=in_specs,
        out_specs=P("prow", "pcol"),
        check_vma=False,
    )
```

```python
import functools

import jax
import jax.numpy as jnp
from jax import lax
from jax.experimental import pallas as pl
from jax.experimental.pallas import tpu as pltpu
from jax.sharding import PartitionSpec as P

BR = 2
BS = 128
SUBS = 4
CAP_L = 19
CAPM = 6
META = 16
RING = 4
CHEAP = pl.CostEstimate(flops=0, bytes_accessed=1024, transcendentals=0)
DEAR = pl.CostEstimate(flops=1 << 35, bytes_accessed=1 << 20, transcendentals=0)
ROOM = pltpu.CompilerParams(vmem_limit_bytes=16 << 20)
SMEM = pl.BlockSpec(memory_space=pltpu.SMEM)
VMEM = pl.BlockSpec(memory_space=pltpu.VMEM)
ANY = pl.BlockSpec(memory_space=pl.ANY)


def by_pairs(array, pairs):
    return lax.ppermute(array, ("prow", "pcol"), pairs)


def stage_kernel(mask_ref, left_ref, right_ref, packed_ref, part_ref, sem, part_sem):
    panel = left_ref.shape[0]
    half = part_ref.shape[0]
    part = pltpu.make_async_copy(right_ref.at[pl.ds(half, half)], part_ref, part_sem)
    part.start()
    slot = jnp.int32(0)
    for q in range(panel):
        taken = jnp.logical_and(mask_ref[q] != 0, slot < CAP_L)

        @pl.when(taken)
        def _(q=q, slot=slot):
            row = pl.multiple_of(slot * BS, BS)
            pltpu.make_async_copy(left_ref.at[q], packed_ref.at[pl.ds(row, BS)], sem).start()

        slot = slot + taken.astype(jnp.int32)

    @pl.loop(slot, CAP_L)
    def _(spare):
        row = pl.multiple_of(spare * BS, BS)
        pltpu.make_async_copy(left_ref.at[0], packed_ref.at[pl.ds(row, BS)], sem).start()

    lane = lax.broadcasted_iota(jnp.int32, (META, BS), 1)
    mask = jnp.zeros((META, BS), jnp.float32)
    for q in range(panel):
        mask = jnp.where(lane == q, (mask_ref[q] != 0).astype(jnp.float32), mask)
    packed_ref[pl.ds(CAP_L * BS, META), :] = mask.astype(packed_ref.dtype)
    blocks = packed_ref.at[pl.ds(0, CAP_L * BS)]
    pltpu.make_async_copy(blocks, blocks, sem).wait()
    part.wait()


def stage(left_mask, left_blocks, right_blocks):
    return pl.pallas_call(
        stage_kernel,
        out_shape=[
            jax.ShapeDtypeStruct((CAP_L * BS + META, BS), jnp.bfloat16),
            jax.ShapeDtypeStruct((2 * CAPM, BS, BS), jnp.bfloat16),
        ],
        in_specs=[SMEM, ANY, ANY],
        out_specs=[VMEM, VMEM],
        scratch_shapes=[pltpu.SemaphoreType.DMA, pltpu.SemaphoreType.DMA],
        compiler_params=pltpu.CompilerParams(vmem_limit_bytes=62 << 20),
        cost_estimate=CHEAP,
        name="pack_and_cut",
    )(left_mask, left_blocks, right_blocks)


def mask_of(packed, panel):
    return packed[CAP_L * BS, :panel].astype(jnp.int32)


def place(u, at, lists_ref, counts_ref, mask_ref, sources, into_ref, rank_ref, sem):
    column = lax.axis_index("pcol")
    run = jnp.int32(0)
    for q in range(mask_ref.shape[0]):
        rank_ref[q] = run
        run = run + (mask_ref[q] != 0).astype(jnp.int32)
    held = [(panel_ref, where(column)) for panel_ref, where in sources]
    total = jnp.int32(0)
    for p in range(lists_ref.shape[3]):
        block = lists_ref[0, u, 0, p]
        slot = lists_ref[0, u, 1, p]
        o = lists_ref[0, u, 2, p]
        live = jnp.logical_and(p < counts_ref[0, u], mask_ref[block] != 0)
        row = pl.multiple_of(jnp.minimum(rank_ref[block], CAP_L - 1) * BS, BS)
        down = pl.multiple_of(o * BS, BS)
        along = pl.multiple_of((at * CAPM + slot) * BS, BS)
        target = into_ref.at[pl.ds(down, BS), pl.ds(along, BS)]
        for panel_ref, here in held:
            taken = jnp.logical_and(live, here)

            @pl.when(taken)
            def _(panel_ref=panel_ref, row=row, target=target):
                pltpu.make_async_copy(panel_ref.at[pl.ds(row, BS)], target, sem).start()

            total = total + taken.astype(jnp.int32)
    return total


def drain(total, panel_ref, into_ref, sem):
    @pl.loop(0, total)
    def _(_):
        one = panel_ref.at[pl.ds(0, BS)]
        pltpu.make_async_copy(one, into_ref.at[pl.ds(0, BS), pl.ds(0, BS)], sem).wait()


def multiply(left_ref, right_ref, total_ref):
    for m in range(right_ref.shape[0]):
        total_ref[...] += jnp.dot(
            left_ref[:, m * BS : (m + 1) * BS], right_ref[m], preferred_element_type=jnp.float32
        )


def one_kernel(
    u, here, lists_ref, counts_ref, mask_ref, panel_ref, right_ref, *refs,
):
    before_ref = refs[0] if len(refs) == 7 else None
    known_ref, left_ref, held_ref, rank_ref, sem, right_sem = refs[-6:]
    fetch_right = pltpu.make_async_copy(
        right_ref.at[pl.ds((u - 2) * CAPM, CAPM)], held_ref, right_sem
    )
    fetch_right.start()
    left_ref[...] = jnp.zeros_like(left_ref)
    source = ((panel_ref, here),)
    total = place(u, 0, lists_ref, counts_ref, mask_ref, source, left_ref, rank_ref, sem)
    drain(total, panel_ref, left_ref, sem)
    fetch_right.wait()
    known_ref[...] = jnp.zeros_like(known_ref) if before_ref is None else before_ref[...]
    multiply(left_ref, held_ref, known_ref)


def one_step(u, here, lists, counts, mask, panel, right, before, cost, name):
    more = [] if before is None else [before]
    return pl.pallas_call(
        functools.partial(one_kernel, u, here),
        out_shape=jax.ShapeDtypeStruct((BR * BS, BS), jnp.float32),
        in_specs=[SMEM] * 3 + [ANY] * 2 + [VMEM] * len(more),
        out_specs=VMEM,
        scratch_shapes=[
            pltpu.VMEM((BR * BS, CAPM * BS), jnp.bfloat16),
            pltpu.VMEM((CAPM, BS, BS), jnp.bfloat16),
            pltpu.SMEM((mask.shape[0],), jnp.int32),
            pltpu.SemaphoreType.DMA,
            pltpu.SemaphoreType.DMA,
        ],
        compiler_params=ROOM,
        cost_estimate=cost,
        name=name,
    )(lists, counts, mask, panel, right, *more)


def late_kernel(
    last, lists_ref, counts_ref, two_mask_ref, one_mask_ref, around_mask_ref,
    two_ref, one_ref, handed_ref, around_ref, right_ref, early_ref,
    laid_ref, known_ref, left_ref, held_ref, rank_ref, sem, right_sem,
):
    laid_ref[...] = jnp.zeros_like(laid_ref)
    two = ((two_ref, lambda c: c >= 0),)
    one = (
        (one_ref, lambda c: lax.rem(c, RING) != 0),
        (handed_ref, lambda c: lax.rem(c, RING) == 0),
    )
    total = place(0, 0, lists_ref, counts_ref, two_mask_ref, two, laid_ref, rank_ref, sem)
    total += place(1, 1, lists_ref, counts_ref, one_mask_ref, one, laid_ref, rank_ref, sem)
    known_ref[...] = early_ref[...]
    drain(total, two_ref, laid_ref, sem)

    @pl.when(lax.axis_index("pcol") == last)
    def _():
        fetch_right = pltpu.make_async_copy(
            right_ref.at[pl.ds(CAPM, CAPM)], held_ref, right_sem
        )
        fetch_right.start()
        left_ref[...] = jnp.zeros_like(left_ref)
        above = ((around_ref, lambda c: c >= 0),)
        count = place(
            3, 0, lists_ref, counts_ref, around_mask_ref, above, left_ref, rank_ref, sem
        )
        drain(count, around_ref, left_ref, sem)
        fetch_right.wait()
        multiply(left_ref, held_ref, known_ref)


def late(last, lists, counts, masks, panels, right, known):
    return pl.pallas_call(
        functools.partial(late_kernel, last),
        out_shape=[
            jax.ShapeDtypeStruct((BR * BS, 2 * CAPM * BS), jnp.bfloat16),
            jax.ShapeDtypeStruct((BR * BS, BS), jnp.float32),
        ],
        in_specs=[SMEM] * 5 + [ANY] * 5 + [VMEM],
        out_specs=[VMEM, VMEM],
        scratch_shapes=[
            pltpu.VMEM((BR * BS, CAPM * BS), jnp.bfloat16),
            pltpu.VMEM((CAPM, BS, BS), jnp.bfloat16),
            pltpu.SMEM((masks[0].shape[0],), jnp.int32),
            pltpu.SemaphoreType.DMA,
            pltpu.SemaphoreType.DMA,
        ],
        compiler_params=ROOM,
        cost_estimate=CHEAP,
        name="lay_below",
    )(lists, counts, *masks, *panels, right, known)


def last_kernel(left_ref, right_ref, known_ref, out_ref):
    new = jnp.dot(left_ref[...], right_ref[...], preferred_element_type=jnp.float32)
    out_ref[...] = (known_ref[...] + new).astype(out_ref.dtype)


def last_product(left, right, known):
    return pl.pallas_call(
        last_kernel,
        out_shape=jax.ShapeDtypeStruct(known.shape, jnp.bfloat16),
        in_specs=[VMEM] * 3,
        out_specs=VMEM,
        compiler_params=ROOM,
        cost_estimate=CHEAP,
        name="last_product",
    )(left, right, known)


def on_device(n_row, n_col, left_blocks, left_mask, right_blocks, pair_lists, pair_counts):
    panel = left_blocks.shape[0]
    last = n_col - 1
    half = 2 * CAPM

    def shift(rows, cols, chosen):
        return [
            (r * n_col + c, (r + rows) % n_row * n_col + (c + cols) % n_col)
            for r in range(n_row)
            for c in range(n_col)
            if chosen(c)
        ]

    packed, sent_right = stage(left_mask, left_blocks, right_blocks)
    two_below = by_pairs(packed, shift(0, 2, lambda c: True))
    right_before = by_pairs(sent_right, shift(1, 0, lambda c: True))
    one_above = by_pairs(packed, shift(0, -1, lambda c: c > 0))
    one_below = by_pairs(packed, shift(0, 1, lambda c: c % RING < RING - 1))
    handed = by_pairs(two_below, shift(0, -1, lambda c: c % RING == 1))
    halfway = by_pairs(one_below, shift(0, -4, lambda c: c == 1))
    around = by_pairs(halfway, shift(0, 2, lambda c: c == last - 2))

    column = lax.axis_index("pcol")
    known = one_step(
        2, lambda c: c >= 0, pair_lists, pair_counts, left_mask, packed, right_blocks, None,
        DEAR, "own_step",
    )
    known = one_step(
        3, lambda c: c < last, pair_lists, pair_counts, mask_of(one_above, panel), one_above,
        right_blocks, known, CHEAP, "step_above",
    )
    mask_one = jnp.where(
        column % RING == 0, mask_of(handed, panel), mask_of(one_below, panel)
    )
    laid, known = late(
        last, pair_lists, pair_counts, [mask_of(two_below, panel), mask_one, mask_of(around, panel)],
        [two_below, one_below, handed, around], right_blocks, known,
    )
    return last_product(laid, right_before.reshape(half * BS, BS), known)


def solution(mesh):
    in_specs = (
        P(("prow", "pcol"), None, None),
        P(("prow", "pcol")),
        P(("prow", "pcol"), None, None),
        P(("prow", "pcol"), None, None, None),
        P(("prow", "pcol"), None),
    )
    return jax.shard_map(
        functools.partial(on_device, mesh.shape["prow"], mesh.shape["pcol"]),
        mesh=mesh,
        in_specs=in_specs,
        out_specs=P("prow", "pcol"),
        check_vma=False,
    )
```

```python
import functools

import jax
import jax.numpy as jnp
from jax import lax
from jax.experimental import pallas as pl
from jax.experimental.pallas import tpu as pltpu
from jax.sharding import PartitionSpec as P

BR = 2
BS = 128
CAP_L = 19
CAPM = 6
PCAP = 12
META = 16
RING = 4
CHEAP = pl.CostEstimate(flops=0, bytes_accessed=1024, transcendentals=0)
DEAR = pl.CostEstimate(flops=1 << 35, bytes_accessed=1 << 20, transcendentals=0)
ROOM = pltpu.CompilerParams(vmem_limit_bytes=16 << 20)
WIDE = pltpu.CompilerParams(vmem_limit_bytes=62 << 20)
SMEM = pl.BlockSpec(memory_space=pltpu.SMEM)
VMEM = pl.BlockSpec(memory_space=pltpu.VMEM)
ANY = pl.BlockSpec(memory_space=pl.ANY)


def by_pairs(array, pairs):
    return lax.ppermute(array, ("prow", "pcol"), pairs)


def pack_into(mask_ref, left_ref, packed_ref, sem):
    panel = left_ref.shape[0]
    slot = jnp.int32(0)
    for q in range(panel):
        taken = jnp.logical_and(mask_ref[q] != 0, slot < CAP_L)

        @pl.when(taken)
        def _(q=q, slot=slot):
            row = pl.multiple_of(slot * BS, BS)
            pltpu.make_async_copy(left_ref.at[q], packed_ref.at[pl.ds(row, BS)], sem).start()

        slot = slot + taken.astype(jnp.int32)

    @pl.loop(slot, CAP_L)
    def _(spare):
        row = pl.multiple_of(spare * BS, BS)
        pltpu.make_async_copy(left_ref.at[0], packed_ref.at[pl.ds(row, BS)], sem).start()

    lane = lax.broadcasted_iota(jnp.int32, (META, BS), 1)
    mask = jnp.zeros((META, BS), jnp.float32)
    for q in range(panel):
        mask = jnp.where(lane == q, (mask_ref[q] != 0).astype(jnp.float32), mask)
    packed_ref[pl.ds(CAP_L * BS, META), :] = mask.astype(packed_ref.dtype)


def wait_packed(packed_ref, sem):
    blocks = packed_ref.at[pl.ds(0, CAP_L * BS)]
    pltpu.make_async_copy(blocks, blocks, sem).wait()


def first_kernel(
    mask_ref, lists_ref, counts_ref, left_ref, right_ref,
    packed_ref, part_ref, ask_ref, sem, part_sem, ask_sem,
):
    half = part_ref.shape[0]
    part = pltpu.make_async_copy(right_ref.at[pl.ds(half, half)], part_ref, part_sem)
    part.start()
    pack_into(mask_ref, left_ref, packed_ref, sem)
    copies = []
    for m in range(CAPM):
        target = ask_ref.at[pl.ds(m * BS, BS)]
        copies.append(pltpu.make_async_copy(right_ref.at[CAPM + m], target, ask_sem.at[m]))
        copies[-1].start()
    lane = lax.broadcasted_iota(jnp.int32, (META, BS), 1)
    pairs = lists_ref.shape[3]
    row = jnp.where(lane == 3 * pairs, counts_ref[0, 3].astype(jnp.float32), 0.0)
    for q in range(3 * pairs):
        row = jnp.where(lane == q, lists_ref[0, 3, q // pairs, q % pairs].astype(jnp.float32), row)
    ask_ref[pl.ds(CAPM * BS, META), :] = row.astype(ask_ref.dtype)
    wait_packed(packed_ref, sem)
    part.wait()
    for copy in copies:
        copy.wait()


def first_stage(left_mask, lists, counts, left_blocks, right_blocks):
    return pl.pallas_call(
        first_kernel,
        out_shape=[
            jax.ShapeDtypeStruct((CAP_L * BS + META, BS), jnp.bfloat16),
            jax.ShapeDtypeStruct((2 * CAPM, BS, BS), jnp.bfloat16),
            jax.ShapeDtypeStruct((CAPM * BS + META, BS), jnp.bfloat16),
        ],
        in_specs=[SMEM] * 3 + [ANY] * 2,
        out_specs=[VMEM] * 3,
        scratch_shapes=[
            pltpu.SemaphoreType.DMA, pltpu.SemaphoreType.DMA, pltpu.SemaphoreType.DMA((CAPM,))
        ],
        compiler_params=WIDE,
        cost_estimate=CHEAP,
        name="pack_and_cut",
    )(left_mask, lists, counts, left_blocks, right_blocks)


def mask_of(packed, panel):
    return packed[CAP_L * BS, :panel].astype(jnp.int32)


def place(u, at, lists_ref, counts_ref, mask_ref, sources, into_ref, rank_ref, sem):
    column = lax.axis_index("pcol")
    run = jnp.int32(0)
    for q in range(mask_ref.shape[0]):
        rank_ref[q] = run
        run = run + (mask_ref[q] != 0).astype(jnp.int32)
    held = [(panel_ref, where(column)) for panel_ref, where in sources]
    total = jnp.int32(0)
    for p in range(lists_ref.shape[3]):
        block = lists_ref[0, u, 0, p]
        slot = lists_ref[0, u, 1, p]
        o = lists_ref[0, u, 2, p]
        live = jnp.logical_and(p < counts_ref[0, u], mask_ref[block] != 0)
        row = pl.multiple_of(jnp.minimum(rank_ref[block], CAP_L - 1) * BS, BS)
        down = pl.multiple_of(o * BS, BS)
        along = pl.multiple_of((at * CAPM + slot) * BS, BS)
        target = into_ref.at[pl.ds(down, BS), pl.ds(along, BS)]
        for panel_ref, here in held:
            taken = jnp.logical_and(live, here)

            @pl.when(taken)
            def _(panel_ref=panel_ref, row=row, target=target):
                pltpu.make_async_copy(panel_ref.at[pl.ds(row, BS)], target, sem).start()

            total = total + taken.astype(jnp.int32)
    return total


def drain(total, panel_ref, into_ref, sem):
    @pl.loop(0, total)
    def _(_):
        one = panel_ref.at[pl.ds(0, BS)]
        pltpu.make_async_copy(one, into_ref.at[pl.ds(0, BS), pl.ds(0, BS)], sem).wait()


def multiply(left_ref, right_ref, total_ref):
    for m in range(right_ref.shape[0]):
        total_ref[...] += jnp.dot(
            left_ref[:, m * BS : (m + 1) * BS], right_ref[m], preferred_element_type=jnp.float32
        )


def one_kernel(
    u, first, here, lists_ref, counts_ref, mask_ref, panel_ref, right_ref, *refs,
):
    before_ref = refs[0] if len(refs) == 7 else None
    known_ref, left_ref, held_ref, rank_ref, sem, right_sem = refs[-6:]
    fetch_right = pltpu.make_async_copy(
        right_ref.at[pl.ds(first, CAPM)], held_ref, right_sem
    )
    fetch_right.start()
    left_ref[...] = jnp.zeros_like(left_ref)
    source = ((panel_ref, here),)
    total = place(u, 0, lists_ref, counts_ref, mask_ref, source, left_ref, rank_ref, sem)
    drain(total, panel_ref, left_ref, sem)
    fetch_right.wait()
    known_ref[...] = jnp.zeros_like(known_ref) if before_ref is None else before_ref[...]
    multiply(left_ref, held_ref, known_ref)


def one_step(u, first, here, lists, counts, mask, panel, right, before, cost, name):
    more = [] if before is None else [before]
    return pl.pallas_call(
        functools.partial(one_kernel, u, first, here),
        out_shape=jax.ShapeDtypeStruct((BR * BS, BS), jnp.float32),
        in_specs=[SMEM] * 3 + [ANY] * 2 + [VMEM] * len(more),
        out_specs=VMEM,
        scratch_shapes=[
            pltpu.VMEM((BR * BS, CAPM * BS), jnp.bfloat16),
            pltpu.VMEM((CAPM, BS, BS), jnp.bfloat16),
            pltpu.SMEM((mask.shape[0],), jnp.int32),
            pltpu.SemaphoreType.DMA,
            pltpu.SemaphoreType.DMA,
        ],
        compiler_params=ROOM,
        cost_estimate=cost,
        name=name,
    )(lists, counts, mask, panel, right, *more)


def late_kernel(
    lists_ref, counts_ref, two_mask_ref, one_mask_ref, two_ref, one_ref, handed_ref,
    early_ref, answer_ref, laid_ref, known_ref, rank_ref, sem,
):
    laid_ref[...] = jnp.zeros_like(laid_ref)
    two = ((two_ref, lambda c: c >= 0),)
    one = (
        (one_ref, lambda c: lax.rem(c, RING) != 0),
        (handed_ref, lambda c: lax.rem(c, RING) == 0),
    )
    total = place(0, 0, lists_ref, counts_ref, two_mask_ref, two, laid_ref, rank_ref, sem)
    total += place(1, 1, lists_ref, counts_ref, one_mask_ref, one, laid_ref, rank_ref, sem)
    known_ref[...] = early_ref[...] + answer_ref[...]
    drain(total, two_ref, laid_ref, sem)


def late(lists, counts, masks, panels, known, answer):
    return pl.pallas_call(
        late_kernel,
        out_shape=[
            jax.ShapeDtypeStruct((BR * BS, 2 * CAPM * BS), jnp.bfloat16),
            jax.ShapeDtypeStruct((BR * BS, BS), jnp.float32),
        ],
        in_specs=[SMEM] * 4 + [ANY] * 3 + [VMEM] * 2,
        out_specs=[VMEM, VMEM],
        scratch_shapes=[pltpu.SMEM((masks[0].shape[0],), jnp.int32), pltpu.SemaphoreType.DMA],
        compiler_params=ROOM,
        cost_estimate=CHEAP,
        name="lay_below",
    )(lists, counts, *masks, *panels, known, answer)


def last_kernel(left_ref, right_ref, known_ref, out_ref):
    new = jnp.dot(left_ref[...], right_ref[...], preferred_element_type=jnp.float32)
    out_ref[...] = (known_ref[...] + new).astype(out_ref.dtype)


def last_product(left, right, known):
    return pl.pallas_call(
        last_kernel,
        out_shape=jax.ShapeDtypeStruct(known.shape, jnp.bfloat16),
        in_specs=[VMEM] * 3,
        out_specs=VMEM,
        compiler_params=ROOM,
        cost_estimate=CHEAP,
        name="last_product",
    )(left, right, known)


def on_device(n_row, n_col, left_blocks, left_mask, right_blocks, pair_lists, pair_counts):
    panel = left_blocks.shape[0]
    last = n_col - 1
    half = 2 * CAPM

    def shift(rows, cols, chosen):
        return [
            (r * n_col + c, (r + rows) % n_row * n_col + (c + cols) % n_col)
            for r in range(n_row)
            for c in range(n_col)
            if chosen(c)
        ]

    def always(c):
        return c >= 0

    packed, sent_right, ask = first_stage(
        left_mask, pair_lists, pair_counts, left_blocks, right_blocks
    )
    two_below = by_pairs(packed, shift(0, 2, always))
    right_before = by_pairs(sent_right, shift(1, 0, always))
    one_above = by_pairs(packed, shift(0, -1, lambda c: c > 0))
    one_below = by_pairs(packed, shift(0, 1, lambda c: c % RING < RING - 1))
    asked = by_pairs(ask, shift(0, 1, lambda c: c == last))
    handed = by_pairs(two_below, shift(0, -1, lambda c: c % RING == 1))

    listed = asked[CAPM * BS, : 3 * PCAP + 1].astype(jnp.int32)
    answer = one_step(
        0, 0, always, listed[: 3 * PCAP].reshape(1, 1, 3, PCAP), listed[3 * PCAP :].reshape(1, 1),
        left_mask, packed, asked[: CAPM * BS].reshape(CAPM, BS, BS), None, CHEAP, "answer",
    )
    answer = by_pairs(answer, shift(0, -3, lambda c: c == 0))
    answer = by_pairs(answer, shift(0, 2, lambda c: c == last - 2))

    known = one_step(
        2, 0, always, pair_lists, pair_counts, left_mask, packed, right_blocks, None,
        DEAR, "own_step",
    )
    known = one_step(
        3, CAPM, lambda c: c < last, pair_lists, pair_counts, mask_of(one_above, panel),
        one_above, right_blocks, known, DEAR, "step_above",
    )
    first = lax.axis_index("pcol") % RING == 0
    mask_one = jnp.where(first, mask_of(handed, panel), mask_of(one_below, panel))
    laid, known = late(
        pair_lists, pair_counts, [mask_of(two_below, panel), mask_one],
        [two_below, one_below, handed], known, answer,
    )
    return last_product(laid, right_before.reshape(half * BS, BS), known)


def solution(mesh):
    in_specs = (
        P(("prow", "pcol"), None, None),
        P(("prow", "pcol")),
        P(("prow", "pcol"), None, None),
        P(("prow", "pcol"), None, None, None),
        P(("prow", "pcol"), None),
    )
    return jax.shard_map(
        functools.partial(on_device, mesh.shape["prow"], mesh.shape["pcol"]),
        mesh=mesh,
        in_specs=in_specs,
        out_specs=P("prow", "pcol"),
        check_vma=False,
    )
```

```python
import functools

import jax
import jax.numpy as jnp
from jax import lax
from jax.experimental import pallas as pl
from jax.experimental.pallas import tpu as pltpu
from jax.sharding import PartitionSpec as P

BR = 2
BS = 128
CAP_L = 19
CAPM = 6
META = 16
RING = 4
CHEAP = pl.CostEstimate(flops=0, bytes_accessed=1024, transcendentals=0)
DEAR = pl.CostEstimate(flops=1 << 35, bytes_accessed=1 << 20, transcendentals=0)
ROOM = pltpu.CompilerParams(vmem_limit_bytes=16 << 20)
WIDE = pltpu.CompilerParams(vmem_limit_bytes=62 << 20)
SMEM = pl.BlockSpec(memory_space=pltpu.SMEM)
VMEM = pl.BlockSpec(memory_space=pltpu.VMEM)
ANY = pl.BlockSpec(memory_space=pl.ANY)


def by_pairs(array, pairs):
    return lax.ppermute(array, ("prow", "pcol"), pairs)


def pack_into(mask_ref, left_ref, packed_ref, sem):
    panel = left_ref.shape[0]
    slot = jnp.int32(0)
    for q in range(panel):
        taken = jnp.logical_and(mask_ref[q] != 0, slot < CAP_L)

        @pl.when(taken)
        def _(q=q, slot=slot):
            row = pl.multiple_of(slot * BS, BS)
            pltpu.make_async_copy(left_ref.at[q], packed_ref.at[pl.ds(row, BS)], sem).start()

        slot = slot + taken.astype(jnp.int32)

    @pl.loop(slot, CAP_L)
    def _(spare):
        row = pl.multiple_of(spare * BS, BS)
        pltpu.make_async_copy(left_ref.at[0], packed_ref.at[pl.ds(row, BS)], sem).start()

    lane = lax.broadcasted_iota(jnp.int32, (META, BS), 1)
    mask = jnp.zeros((META, BS), jnp.float32)
    for q in range(panel):
        mask = jnp.where(lane == q, (mask_ref[q] != 0).astype(jnp.float32), mask)
    packed_ref[pl.ds(CAP_L * BS, META), :] = mask.astype(packed_ref.dtype)


def wait_packed(packed_ref, sem):
    blocks = packed_ref.at[pl.ds(0, CAP_L * BS)]
    pltpu.make_async_copy(blocks, blocks, sem).wait()


def first_kernel(mask_ref, left_ref, right_ref, packed_ref, part_ref, sem, part_sem):
    half = part_ref.shape[0]
    part = pltpu.make_async_copy(right_ref.at[pl.ds(half, half)], part_ref, part_sem)
    part.start()
    pack_into(mask_ref, left_ref, packed_ref, sem)
    wait_packed(packed_ref, sem)
    part.wait()


def first_stage(left_mask, left_blocks, right_blocks):
    return pl.pallas_call(
        first_kernel,
        out_shape=[
            jax.ShapeDtypeStruct((CAP_L * BS + META, BS), jnp.bfloat16),
            jax.ShapeDtypeStruct((2 * CAPM, BS, BS), jnp.bfloat16),
        ],
        in_specs=[SMEM, ANY, ANY],
        out_specs=[VMEM, VMEM],
        scratch_shapes=[pltpu.SemaphoreType.DMA, pltpu.SemaphoreType.DMA],
        compiler_params=WIDE,
        cost_estimate=CHEAP,
        name="pack_and_cut",
    )(left_mask, left_blocks, right_blocks)


def pack_kernel(mask_ref, left_ref, after_ref, packed_ref, sem):
    del after_ref
    pack_into(mask_ref, left_ref, packed_ref, sem)
    wait_packed(packed_ref, sem)


def pack(left_mask, left_blocks, after, name):
    return pl.pallas_call(
        pack_kernel,
        out_shape=jax.ShapeDtypeStruct((CAP_L * BS + META, BS), jnp.bfloat16),
        in_specs=[SMEM, ANY, ANY],
        out_specs=VMEM,
        scratch_shapes=[pltpu.SemaphoreType.DMA],
        compiler_params=WIDE,
        cost_estimate=CHEAP,
        name=name,
    )(left_mask, left_blocks, after)


def mask_of(packed, panel):
    return packed[CAP_L * BS, :panel].astype(jnp.int32)


def place(u, at, lists_ref, counts_ref, mask_ref, sources, into_ref, rank_ref, sem):
    column = lax.axis_index("pcol")
    run = jnp.int32(0)
    for q in range(mask_ref.shape[0]):
        rank_ref[q] = run
        run = run + (mask_ref[q] != 0).astype(jnp.int32)
    held = [(panel_ref, where(column)) for panel_ref, where in sources]
    total = jnp.int32(0)
    for p in range(lists_ref.shape[3]):
        block = lists_ref[0, u, 0, p]
        slot = lists_ref[0, u, 1, p]
        o = lists_ref[0, u, 2, p]
        live = jnp.logical_and(p < counts_ref[0, u], mask_ref[block] != 0)
        row = pl.multiple_of(jnp.minimum(rank_ref[block], CAP_L - 1) * BS, BS)
        down = pl.multiple_of(o * BS, BS)
        along = pl.multiple_of((at * CAPM + slot) * BS, BS)
        target = into_ref.at[pl.ds(down, BS), pl.ds(along, BS)]
        for panel_ref, here in held:
            taken = jnp.logical_and(live, here)

            @pl.when(taken)
            def _(panel_ref=panel_ref, row=row, target=target):
                pltpu.make_async_copy(panel_ref.at[pl.ds(row, BS)], target, sem).start()

            total = total + taken.astype(jnp.int32)
    return total


def drain(total, panel_ref, into_ref, sem):
    @pl.loop(0, total)
    def _(_):
        one = panel_ref.at[pl.ds(0, BS)]
        pltpu.make_async_copy(one, into_ref.at[pl.ds(0, BS), pl.ds(0, BS)], sem).wait()


def multiply(left_ref, right_ref, total_ref):
    for m in range(right_ref.shape[0]):
        total_ref[...] += jnp.dot(
            left_ref[:, m * BS : (m + 1) * BS], right_ref[m], preferred_element_type=jnp.float32
        )


def one_kernel(
    u, first, here, lists_ref, counts_ref, mask_ref, panel_ref, right_ref, *refs,
):
    before_ref = refs[0] if len(refs) == 7 else None
    known_ref, left_ref, held_ref, rank_ref, sem, right_sem = refs[-6:]
    fetch_right = pltpu.make_async_copy(
        right_ref.at[pl.ds(first, CAPM)], held_ref, right_sem
    )
    fetch_right.start()
    left_ref[...] = jnp.zeros_like(left_ref)
    source = ((panel_ref, here),)
    total = place(u, 0, lists_ref, counts_ref, mask_ref, source, left_ref, rank_ref, sem)
    drain(total, panel_ref, left_ref, sem)
    fetch_right.wait()
    known_ref[...] = jnp.zeros_like(known_ref) if before_ref is None else before_ref[...]
    multiply(left_ref, held_ref, known_ref)


def one_step(u, first, here, lists, counts, mask, panel, right, before, cost, name):
    more = [] if before is None else [before]
    return pl.pallas_call(
        functools.partial(one_kernel, u, first, here),
        out_shape=jax.ShapeDtypeStruct((BR * BS, BS), jnp.float32),
        in_specs=[SMEM] * 3 + [ANY] * 2 + [VMEM] * len(more),
        out_specs=VMEM,
        scratch_shapes=[
            pltpu.VMEM((BR * BS, CAPM * BS), jnp.bfloat16),
            pltpu.VMEM((CAPM, BS, BS), jnp.bfloat16),
            pltpu.SMEM((mask.shape[0],), jnp.int32),
            pltpu.SemaphoreType.DMA,
            pltpu.SemaphoreType.DMA,
        ],
        compiler_params=ROOM,
        cost_estimate=cost,
        name=name,
    )(lists, counts, mask, panel, right, *more)


def late_kernel(
    lists_ref, counts_ref, two_mask_ref, one_mask_ref, two_ref, one_ref, handed_ref,
    laid_ref, rank_ref, sem,
):
    laid_ref[...] = jnp.zeros_like(laid_ref)
    two = ((two_ref, lambda c: c >= 0),)
    one = (
        (one_ref, lambda c: lax.rem(c, RING) != 0),
        (handed_ref, lambda c: lax.rem(c, RING) == 0),
    )
    total = place(0, 0, lists_ref, counts_ref, two_mask_ref, two, laid_ref, rank_ref, sem)
    total += place(1, 1, lists_ref, counts_ref, one_mask_ref, one, laid_ref, rank_ref, sem)
    drain(total, two_ref, laid_ref, sem)


def late(lists, counts, masks, panels):
    return pl.pallas_call(
        late_kernel,
        out_shape=jax.ShapeDtypeStruct((BR * BS, 2 * CAPM * BS), jnp.bfloat16),
        in_specs=[SMEM] * 4 + [ANY] * 3,
        out_specs=VMEM,
        scratch_shapes=[pltpu.SMEM((masks[0].shape[0],), jnp.int32), pltpu.SemaphoreType.DMA],
        compiler_params=ROOM,
        cost_estimate=CHEAP,
        name="lay_below",
    )(lists, counts, *masks, *panels)


def last_kernel(known_ref, left_ref, right_ref, out_ref):
    new = jnp.dot(left_ref[...], right_ref[...], preferred_element_type=jnp.float32)
    out_ref[...] = (known_ref[...] + new).astype(out_ref.dtype)


def last_product(known, left, right):
    return pl.pallas_call(
        last_kernel,
        out_shape=jax.ShapeDtypeStruct(known.shape, jnp.bfloat16),
        in_specs=[VMEM] * 3,
        out_specs=VMEM,
        compiler_params=ROOM,
        cost_estimate=CHEAP,
        name="last_product",
    )(known, left, right)


def on_device(n_row, n_col, left_blocks, left_mask, right_blocks, pair_lists, pair_counts):
    panel = left_blocks.shape[0]
    half = 2 * CAPM

    def shift(rows, cols, chosen):
        return [
            (r * n_col + c, (r + rows) % n_row * n_col + (c + cols) % n_col)
            for r in range(n_row)
            for c in range(n_col)
            if chosen(c)
        ]

    def always(c):
        return c >= 0

    packed, sent_right = first_stage(left_mask, left_blocks, right_blocks)
    two_below = by_pairs(packed, shift(0, 2, always))
    right_before = by_pairs(sent_right, shift(1, 0, always))
    mark = by_pairs(left_mask, [(0, 1)])
    again = pack(left_mask, left_blocks, mark, "pack_again")
    one_above = by_pairs(again, shift(0, -1, always))
    one_below = by_pairs(again, shift(0, 1, lambda c: c % RING < RING - 1))
    handed = by_pairs(two_below, shift(0, -1, lambda c: c % RING == 1))

    known = one_step(
        2, 0, always, pair_lists, pair_counts, left_mask, packed, right_blocks, None,
        DEAR, "own_step",
    )
    known = one_step(
        3, CAPM, always, pair_lists, pair_counts, mask_of(one_above, panel),
        one_above, right_blocks, known, CHEAP, "step_above",
    )
    first = lax.axis_index("pcol") % RING == 0
    mask_one = jnp.where(first, mask_of(handed, panel), mask_of(one_below, panel))
    laid = late(
        pair_lists, pair_counts, [mask_of(two_below, panel), mask_one],
        [two_below, one_below, handed],
    )
    return last_product(known, laid, right_before.reshape(half * BS, BS))


def solution(mesh):
    in_specs = (
        P(("prow", "pcol"), None, None),
        P(("prow", "pcol")),
        P(("prow", "pcol"), None, None),
        P(("prow", "pcol"), None, None, None),
        P(("prow", "pcol"), None),
    )
    return jax.shard_map(
        functools.partial(on_device, mesh.shape["prow"], mesh.shape["pcol"]),
        mesh=mesh,
        in_specs=in_specs,
        out_specs=P("prow", "pcol"),
        check_vma=False,
    )
```

```python
import functools

import jax
import jax.numpy as jnp
from jax import lax
from jax.experimental import pallas as pl
from jax.experimental.pallas import tpu as pltpu
from jax.sharding import PartitionSpec as P

BR = 2
BS = 128
CAP_L = 19
CAPM = 6
META = 16
RING = 4
CHEAP = pl.CostEstimate(flops=0, bytes_accessed=1024, transcendentals=0)
DEAR = pl.CostEstimate(flops=1 << 35, bytes_accessed=1 << 20, transcendentals=0)
ROOM = pltpu.CompilerParams(vmem_limit_bytes=16 << 20)
WIDE = pltpu.CompilerParams(vmem_limit_bytes=62 << 20)
SMEM = pl.BlockSpec(memory_space=pltpu.SMEM)
VMEM = pl.BlockSpec(memory_space=pltpu.VMEM)
ANY = pl.BlockSpec(memory_space=pl.ANY)


def by_pairs(array, pairs):
    return lax.ppermute(array, ("prow", "pcol"), pairs)


def pack_into(mask_ref, left_ref, packed_ref, sem):
    panel = left_ref.shape[0]
    slot = jnp.int32(0)
    for q in range(panel):
        taken = jnp.logical_and(mask_ref[q] != 0, slot < CAP_L)

        @pl.when(taken)
        def _(q=q, slot=slot):
            row = pl.multiple_of(slot * BS, BS)
            pltpu.make_async_copy(left_ref.at[q], packed_ref.at[pl.ds(row, BS)], sem).start()

        slot = slot + taken.astype(jnp.int32)

    @pl.loop(slot, CAP_L)
    def _(spare):
        row = pl.multiple_of(spare * BS, BS)
        pltpu.make_async_copy(left_ref.at[0], packed_ref.at[pl.ds(row, BS)], sem).start()

    lane = lax.broadcasted_iota(jnp.int32, (META, BS), 1)
    mask = jnp.zeros((META, BS), jnp.float32)
    for q in range(panel):
        mask = jnp.where(lane == q, (mask_ref[q] != 0).astype(jnp.float32), mask)
    packed_ref[pl.ds(CAP_L * BS, META), :] = mask.astype(packed_ref.dtype)


def wait_packed(packed_ref, sem):
    blocks = packed_ref.at[pl.ds(0, CAP_L * BS)]
    pltpu.make_async_copy(blocks, blocks, sem).wait()


def first_kernel(mask_ref, left_ref, right_ref, packed_ref, part_ref, sem, part_sem):
    half = part_ref.shape[0]
    part = pltpu.make_async_copy(right_ref.at[pl.ds(half, half)], part_ref, part_sem)
    part.start()
    pack_into(mask_ref, left_ref, packed_ref, sem)
    wait_packed(packed_ref, sem)
    part.wait()


def first_stage(left_mask, left_blocks, right_blocks):
    return pl.pallas_call(
        first_kernel,
        out_shape=[
            jax.ShapeDtypeStruct((CAP_L * BS + META, BS), jnp.bfloat16),
            jax.ShapeDtypeStruct((2 * CAPM, BS, BS), jnp.bfloat16),
        ],
        in_specs=[SMEM, ANY, ANY],
        out_specs=[VMEM, VMEM],
        scratch_shapes=[pltpu.SemaphoreType.DMA, pltpu.SemaphoreType.DMA],
        compiler_params=WIDE,
        cost_estimate=CHEAP,
        name="pack_and_cut",
    )(left_mask, left_blocks, right_blocks)


def pack_kernel(mask_ref, left_ref, after_ref, packed_ref, sem):
    del after_ref
    pack_into(mask_ref, left_ref, packed_ref, sem)
    wait_packed(packed_ref, sem)


def pack(left_mask, left_blocks, after, name):
    return pl.pallas_call(
        pack_kernel,
        out_shape=jax.ShapeDtypeStruct((CAP_L * BS + META, BS), jnp.bfloat16),
        in_specs=[SMEM, ANY, ANY],
        out_specs=VMEM,
        scratch_shapes=[pltpu.SemaphoreType.DMA],
        compiler_params=WIDE,
        cost_estimate=CHEAP,
        name=name,
    )(left_mask, left_blocks, after)


def mask_of(packed, panel):
    return packed[CAP_L * BS, :panel].astype(jnp.int32)


def place(u, at, lists_ref, counts_ref, mask_ref, sources, into_ref, rank_ref, sem):
    column = lax.axis_index("pcol")
    run = jnp.int32(0)
    for q in range(mask_ref.shape[0]):
        rank_ref[q] = run
        run = run + (mask_ref[q] != 0).astype(jnp.int32)
    held = [(panel_ref, where(column)) for panel_ref, where in sources]
    total = jnp.int32(0)
    for p in range(lists_ref.shape[3]):
        block = lists_ref[0, u, 0, p]
        slot = lists_ref[0, u, 1, p]
        o = lists_ref[0, u, 2, p]
        live = jnp.logical_and(p < counts_ref[0, u], mask_ref[block] != 0)
        row = pl.multiple_of(jnp.minimum(rank_ref[block], CAP_L - 1) * BS, BS)
        down = pl.multiple_of(o * BS, BS)
        along = pl.multiple_of((at * CAPM + slot) * BS, BS)
        target = into_ref.at[pl.ds(down, BS), pl.ds(along, BS)]
        for panel_ref, here in held:
            taken = jnp.logical_and(live, here)

            @pl.when(taken)
            def _(panel_ref=panel_ref, row=row, target=target):
                pltpu.make_async_copy(panel_ref.at[pl.ds(row, BS)], target, sem).start()

            total = total + taken.astype(jnp.int32)
    return total


def drain(total, panel_ref, into_ref, sem):
    @pl.loop(0, total)
    def _(_):
        one = panel_ref.at[pl.ds(0, BS)]
        pltpu.make_async_copy(one, into_ref.at[pl.ds(0, BS), pl.ds(0, BS)], sem).wait()


def multiply(left_ref, right_ref, total_ref):
    for m in range(right_ref.shape[0]):
        total_ref[...] += jnp.dot(
            left_ref[:, m * BS : (m + 1) * BS], right_ref[m], preferred_element_type=jnp.float32
        )


def one_kernel(
    u, first, here, lists_ref, counts_ref, mask_ref, panel_ref, right_ref, *refs,
):
    before_ref = refs[0] if len(refs) == 8 else None
    known_ref, left_ref, held_ref, rank_ref, sem, right_sem = refs[-6:]
    fetch_right = pltpu.make_async_copy(
        right_ref.at[pl.ds(first, CAPM)], held_ref, right_sem
    )
    fetch_right.start()
    left_ref[...] = jnp.zeros_like(left_ref)
    source = ((panel_ref, here),)
    total = place(u, 0, lists_ref, counts_ref, mask_ref, source, left_ref, rank_ref, sem)
    drain(total, panel_ref, left_ref, sem)
    fetch_right.wait()
    known_ref[...] = jnp.zeros_like(known_ref) if before_ref is None else before_ref[...]
    multiply(left_ref, held_ref, known_ref)


def one_step(u, first, here, lists, counts, mask, panel, right, before, after, cost, name):
    more = [] if before is None else [before, after]
    return pl.pallas_call(
        functools.partial(one_kernel, u, first, here),
        out_shape=jax.ShapeDtypeStruct((BR * BS, BS), jnp.float32),
        in_specs=[SMEM] * 3 + [ANY] * 2 + [VMEM, ANY][: len(more)],
        out_specs=VMEM,
        scratch_shapes=[
            pltpu.VMEM((BR * BS, CAPM * BS), jnp.bfloat16),
            pltpu.VMEM((CAPM, BS, BS), jnp.bfloat16),
            pltpu.SMEM((mask.shape[0],), jnp.int32),
            pltpu.SemaphoreType.DMA,
            pltpu.SemaphoreType.DMA,
        ],
        compiler_params=ROOM,
        cost_estimate=cost,
        name=name,
    )(lists, counts, mask, panel, right, *more)


def late_kernel(
    lists_ref, counts_ref, two_mask_ref, one_mask_ref, two_ref, one_ref, handed_ref,
    laid_ref, rank_ref, sem,
):
    laid_ref[...] = jnp.zeros_like(laid_ref)
    two = ((two_ref, lambda c: c >= 0),)
    one = (
        (one_ref, lambda c: lax.rem(c, RING) != 0),
        (handed_ref, lambda c: lax.rem(c, RING) == 0),
    )
    total = place(0, 0, lists_ref, counts_ref, two_mask_ref, two, laid_ref, rank_ref, sem)
    total += place(1, 1, lists_ref, counts_ref, one_mask_ref, one, laid_ref, rank_ref, sem)
    drain(total, two_ref, laid_ref, sem)


def late(lists, counts, masks, panels):
    return pl.pallas_call(
        late_kernel,
        out_shape=jax.ShapeDtypeStruct((BR * BS, 2 * CAPM * BS), jnp.bfloat16),
        in_specs=[SMEM] * 4 + [ANY] * 3,
        out_specs=VMEM,
        scratch_shapes=[pltpu.SMEM((masks[0].shape[0],), jnp.int32), pltpu.SemaphoreType.DMA],
        compiler_params=ROOM,
        cost_estimate=CHEAP,
        name="lay_below",
    )(lists, counts, *masks, *panels)


def last_kernel(known_ref, left_ref, right_ref, out_ref):
    new = jnp.dot(left_ref[...], right_ref[...], preferred_element_type=jnp.float32)
    out_ref[...] = (known_ref[...] + new).astype(out_ref.dtype)


def last_product(known, left, right):
    return pl.pallas_call(
        last_kernel,
        out_shape=jax.ShapeDtypeStruct(known.shape, jnp.bfloat16),
        in_specs=[VMEM] * 3,
        out_specs=VMEM,
        compiler_params=ROOM,
        cost_estimate=CHEAP,
        name="last_product",
    )(known, left, right)


def on_device(n_row, n_col, left_blocks, left_mask, right_blocks, pair_lists, pair_counts):
    panel = left_blocks.shape[0]
    half = 2 * CAPM

    def shift(rows, cols, chosen):
        return [
            (r * n_col + c, (r + rows) % n_row * n_col + (c + cols) % n_col)
            for r in range(n_row)
            for c in range(n_col)
            if chosen(c)
        ]

    def always(c):
        return c >= 0

    packed, sent_right = first_stage(left_mask, left_blocks, right_blocks)
    two_below = by_pairs(packed, shift(0, 2, always))
    right_before = by_pairs(sent_right, shift(1, 0, always))
    mark = by_pairs(left_mask, [(0, 1)])
    again = pack(left_mask, left_blocks, mark, "pack_again")
    one_above = by_pairs(again, shift(0, -1, always))
    one_below = by_pairs(again, shift(0, 1, lambda c: c % RING < RING - 1))
    handed = by_pairs(two_below, shift(0, -1, lambda c: c % RING == 1))

    known = one_step(
        2, 0, always, pair_lists, pair_counts, left_mask, packed, right_blocks, None,
        None, DEAR, "own_step",
    )
    first = lax.axis_index("pcol") % RING == 0
    mask_one = jnp.where(first, mask_of(handed, panel), mask_of(one_below, panel))
    laid = late(
        pair_lists, pair_counts, [mask_of(two_below, panel), mask_one],
        [two_below, one_below, handed],
    )
    ordered = laid[0, :panel] * jnp.bfloat16(0)
    mask_above = (one_above[CAP_L * BS, :panel] + ordered).astype(jnp.int32)
    known = one_step(
        3, CAPM, always, pair_lists, pair_counts, mask_above,
        one_above, right_blocks, known, laid, CHEAP, "step_above",
    )
    return last_product(known, laid, right_before.reshape(half * BS, BS))


def solution(mesh):
    in_specs = (
        P(("prow", "pcol"), None, None),
        P(("prow", "pcol")),
        P(("prow", "pcol"), None, None),
        P(("prow", "pcol"), None, None, None),
        P(("prow", "pcol"), None),
    )
    return jax.shard_map(
        functools.partial(on_device, mesh.shape["prow"], mesh.shape["pcol"]),
        mesh=mesh,
        in_specs=in_specs,
        out_specs=P("prow", "pcol"),
        check_vma=False,
    )
```

```python
import functools

import jax
import jax.numpy as jnp
from jax import lax
from jax.experimental import pallas as pl
from jax.experimental.pallas import tpu as pltpu
from jax.sharding import PartitionSpec as P

BR = 2
BS = 128
CAP_L = 19
CAPM = 6
META = 16
RING = 4
CHEAP = pl.CostEstimate(flops=0, bytes_accessed=1024, transcendentals=0)
DEAR = pl.CostEstimate(flops=1 << 35, bytes_accessed=1 << 20, transcendentals=0)
ROOM = pltpu.CompilerParams(vmem_limit_bytes=16 << 20)
WIDE = pltpu.CompilerParams(vmem_limit_bytes=62 << 20)
SMEM = pl.BlockSpec(memory_space=pltpu.SMEM)
VMEM = pl.BlockSpec(memory_space=pltpu.VMEM)
ANY = pl.BlockSpec(memory_space=pl.ANY)


def by_pairs(array, pairs):
    return lax.ppermute(array, ("prow", "pcol"), pairs)


def pack_into(mask_ref, left_ref, packed_ref, sem):
    panel = left_ref.shape[0]
    slot = jnp.int32(0)
    for q in range(panel):
        taken = jnp.logical_and(mask_ref[q] != 0, slot < CAP_L)

        @pl.when(taken)
        def _(q=q, slot=slot):
            row = pl.multiple_of(slot * BS, BS)
            pltpu.make_async_copy(left_ref.at[q], packed_ref.at[pl.ds(row, BS)], sem).start()

        slot = slot + taken.astype(jnp.int32)

    @pl.loop(slot, CAP_L)
    def _(spare):
        row = pl.multiple_of(spare * BS, BS)
        pltpu.make_async_copy(left_ref.at[0], packed_ref.at[pl.ds(row, BS)], sem).start()

    lane = lax.broadcasted_iota(jnp.int32, (META, BS), 1)
    mask = jnp.zeros((META, BS), jnp.float32)
    for q in range(panel):
        mask = jnp.where(lane == q, (mask_ref[q] != 0).astype(jnp.float32), mask)
    packed_ref[pl.ds(CAP_L * BS, META), :] = mask.astype(packed_ref.dtype)


def wait_packed(packed_ref, sem):
    blocks = packed_ref.at[pl.ds(0, CAP_L * BS)]
    pltpu.make_async_copy(blocks, blocks, sem).wait()


def first_kernel(mask_ref, left_ref, right_ref, packed_ref, part_ref, sem, part_sem):
    half = part_ref.shape[0]
    part = pltpu.make_async_copy(right_ref.at[pl.ds(half, half)], part_ref, part_sem)
    part.start()
    pack_into(mask_ref, left_ref, packed_ref, sem)
    wait_packed(packed_ref, sem)
    part.wait()


def first_stage(left_mask, left_blocks, right_blocks):
    return pl.pallas_call(
        first_kernel,
        out_shape=[
            jax.ShapeDtypeStruct((CAP_L * BS + META, BS), jnp.bfloat16),
            jax.ShapeDtypeStruct((2 * CAPM, BS, BS), jnp.bfloat16),
        ],
        in_specs=[SMEM, ANY, ANY],
        out_specs=[VMEM, VMEM],
        scratch_shapes=[pltpu.SemaphoreType.DMA, pltpu.SemaphoreType.DMA],
        compiler_params=WIDE,
        cost_estimate=CHEAP,
        name="pack_and_cut",
    )(left_mask, left_blocks, right_blocks)


def pack_kernel(mask_ref, left_ref, after_ref, packed_ref, sem):
    del after_ref
    pack_into(mask_ref, left_ref, packed_ref, sem)
    wait_packed(packed_ref, sem)


def pack(left_mask, left_blocks, after, name):
    return pl.pallas_call(
        pack_kernel,
        out_shape=jax.ShapeDtypeStruct((CAP_L * BS + META, BS), jnp.bfloat16),
        in_specs=[SMEM, ANY, ANY],
        out_specs=VMEM,
        scratch_shapes=[pltpu.SemaphoreType.DMA],
        compiler_params=WIDE,
        cost_estimate=CHEAP,
        name=name,
    )(left_mask, left_blocks, after)


def mask_of(packed, panel):
    return packed[CAP_L * BS, :panel].astype(jnp.int32)


def place(u, at, lists_ref, counts_ref, mask_ref, sources, into_ref, rank_ref, sem):
    column = lax.axis_index("pcol")
    run = jnp.int32(0)
    for q in range(mask_ref.shape[0]):
        rank_ref[q] = run
        run = run + (mask_ref[q] != 0).astype(jnp.int32)
    held = [(panel_ref, where(column)) for panel_ref, where in sources]
    total = jnp.int32(0)
    for p in range(lists_ref.shape[3]):
        block = lists_ref[0, u, 0, p]
        slot = lists_ref[0, u, 1, p]
        o = lists_ref[0, u, 2, p]
        live = jnp.logical_and(p < counts_ref[0, u], mask_ref[block] != 0)
        row = pl.multiple_of(jnp.minimum(rank_ref[block], CAP_L - 1) * BS, BS)
        down = pl.multiple_of(o * BS, BS)
        along = pl.multiple_of((at * CAPM + slot) * BS, BS)
        target = into_ref.at[pl.ds(down, BS), pl.ds(along, BS)]
        for panel_ref, here in held:
            taken = jnp.logical_and(live, here)

            @pl.when(taken)
            def _(panel_ref=panel_ref, row=row, target=target):
                pltpu.make_async_copy(panel_ref.at[pl.ds(row, BS)], target, sem).start()

            total = total + taken.astype(jnp.int32)
    return total


def drain(total, panel_ref, into_ref, sem):
    @pl.loop(0, total)
    def _(_):
        one = panel_ref.at[pl.ds(0, BS)]
        pltpu.make_async_copy(one, into_ref.at[pl.ds(0, BS), pl.ds(0, BS)], sem).wait()


def multiply(left_ref, right_ref, total_ref):
    for m in range(right_ref.shape[0]):
        total_ref[...] += jnp.dot(
            left_ref[:, m * BS : (m + 1) * BS], right_ref[m], preferred_element_type=jnp.float32
        )


def one_kernel(
    u, first, here, lists_ref, counts_ref, mask_ref, panel_ref, right_ref, *refs,
):
    before_ref = refs[0] if len(refs) == 8 else None
    known_ref, left_ref, held_ref, rank_ref, sem, right_sem = refs[-6:]
    fetch_right = pltpu.make_async_copy(
        right_ref.at[pl.ds(first, CAPM)], held_ref, right_sem
    )
    fetch_right.start()
    left_ref[...] = jnp.zeros_like(left_ref)
    source = ((panel_ref, here),)
    total = place(u, 0, lists_ref, counts_ref, mask_ref, source, left_ref, rank_ref, sem)
    drain(total, panel_ref, left_ref, sem)
    fetch_right.wait()
    known_ref[...] = jnp.zeros_like(known_ref) if before_ref is None else before_ref[...]
    multiply(left_ref, held_ref, known_ref)


def one_step(u, first, here, lists, counts, mask, panel, right, before, after, cost, name):
    more = [] if before is None else [before, after]
    return pl.pallas_call(
        functools.partial(one_kernel, u, first, here),
        out_shape=jax.ShapeDtypeStruct((BR * BS, BS), jnp.float32),
        in_specs=[SMEM] * 3 + [ANY] * 2 + [VMEM, ANY][: len(more)],
        out_specs=VMEM,
        scratch_shapes=[
            pltpu.VMEM((BR * BS, CAPM * BS), jnp.bfloat16),
            pltpu.VMEM((CAPM, BS, BS), jnp.bfloat16),
            pltpu.SMEM((mask.shape[0],), jnp.int32),
            pltpu.SemaphoreType.DMA,
            pltpu.SemaphoreType.DMA,
        ],
        compiler_params=ROOM,
        cost_estimate=cost,
        name=name,
    )(lists, counts, mask, panel, right, *more)


def late_kernel(
    lists_ref, counts_ref, two_mask_ref, one_mask_ref, two_ref, one_ref, handed_ref,
    laid_ref, rank_ref, sem,
):
    laid_ref[...] = jnp.zeros_like(laid_ref)
    two = ((two_ref, lambda c: c >= 0),)
    one = (
        (one_ref, lambda c: lax.rem(c, RING) != 0),
        (handed_ref, lambda c: lax.rem(c, RING) == 0),
    )
    total = place(0, 0, lists_ref, counts_ref, two_mask_ref, two, laid_ref, rank_ref, sem)
    total += place(1, 1, lists_ref, counts_ref, one_mask_ref, one, laid_ref, rank_ref, sem)
    drain(total, two_ref, laid_ref, sem)


def late(lists, counts, masks, panels):
    return pl.pallas_call(
        late_kernel,
        out_shape=jax.ShapeDtypeStruct((BR * BS, 2 * CAPM * BS), jnp.bfloat16),
        in_specs=[SMEM] * 4 + [ANY] * 3,
        out_specs=VMEM,
        scratch_shapes=[pltpu.SMEM((masks[0].shape[0],), jnp.int32), pltpu.SemaphoreType.DMA],
        compiler_params=ROOM,
        cost_estimate=CHEAP,
        name="lay_below",
    )(lists, counts, *masks, *panels)


def last_kernel(known_ref, left_ref, right_ref, out_ref):
    new = jnp.dot(left_ref[...], right_ref[...], preferred_element_type=jnp.float32)
    out_ref[...] = (known_ref[...] + new).astype(out_ref.dtype)


def last_product(known, left, right):
    return pl.pallas_call(
        last_kernel,
        out_shape=jax.ShapeDtypeStruct(known.shape, jnp.bfloat16),
        in_specs=[VMEM] * 3,
        out_specs=VMEM,
        compiler_params=ROOM,
        cost_estimate=CHEAP,
        name="last_product",
    )(known, left, right)


def on_device(n_row, n_col, left_blocks, left_mask, right_blocks, pair_lists, pair_counts):
    panel = left_blocks.shape[0]
    half = 2 * CAPM

    def shift(rows, cols, chosen):
        return [
            (r * n_col + c, (r + rows) % n_row * n_col + (c + cols) % n_col)
            for r in range(n_row)
            for c in range(n_col)
            if chosen(c)
        ]

    def always(c):
        return c >= 0

    packed, sent_right = first_stage(left_mask, left_blocks, right_blocks)
    two_below = by_pairs(packed, shift(0, 2, always))
    right_before = by_pairs(sent_right, shift(1, 0, always))
    mark = by_pairs(left_mask, [(n_col // 2, n_col + n_col // 2)])
    again = pack(left_mask, left_blocks, mark, "pack_again")
    one_above = by_pairs(again, shift(0, -1, always))
    one_below = by_pairs(again, shift(0, 1, lambda c: c % RING < RING - 1))
    handed = by_pairs(two_below, shift(0, -1, lambda c: c % RING == 1))

    known = one_step(
        2, 0, always, pair_lists, pair_counts, left_mask, packed, right_blocks, None,
        None, DEAR, "own_step",
    )
    first = lax.axis_index("pcol") % RING == 0
    mask_one = jnp.where(first, mask_of(handed, panel), mask_of(one_below, panel))
    laid = late(
        pair_lists, pair_counts, [mask_of(two_below, panel), mask_one],
        [two_below, one_below, handed],
    )
    ordered = laid[0, :panel] * jnp.bfloat16(0)
    mask_above = (one_above[CAP_L * BS, :panel] + ordered).astype(jnp.int32)
    known = one_step(
        3, CAPM, always, pair_lists, pair_counts, mask_above,
        one_above, right_blocks, known, laid, CHEAP, "step_above",
    )
    return last_product(known, laid, right_before.reshape(half * BS, BS))


def solution(mesh):
    in_specs = (
        P(("prow", "pcol"), None, None),
        P(("prow", "pcol")),
        P(("prow", "pcol"), None, None),
        P(("prow", "pcol"), None, None, None),
        P(("prow", "pcol"), None),
    )
    return jax.shard_map(
        functools.partial(on_device, mesh.shape["prow"], mesh.shape["pcol"]),
        mesh=mesh,
        in_specs=in_specs,
        out_specs=P("prow", "pcol"),
        check_vma=False,
    )
```
